512 devices in a mesh: seq: 64 (over z, x, core), tp: 8 (over y).
Axes of the slice: x: 4, y: 8, z: 8, core: 2. Of those that a mesh axis runs over, the one named last changes fastest.
Arguments:
- queries: bfloat16 [12288, 5120], P('seq', 'tp'), may hold values from -36 to 36
- keys: bfloat16 [12288, 1024], P('seq', 'tp'), may hold values from -4.5 to 4.5
- values: bfloat16 [12288, 1024], P('seq', 'tp'), may hold values from -6 to 6
- doc_ids: int32 [12288], P('seq'), may hold values from 0 to 5, never falling along the last dimension, each value on 1 to 6144 neighbouring positions
- w_out: bfloat16 [5120, 5120], P('tp', 'seq'), may hold values from -0.078125 to 0.078125
Outputs:
- mixed: bfloat16 [12288, 5120], P('seq', 'tp')
The draws below stay inside these ranges and needn't reach their ends.
Inputs may be any that keep to these rules, and one draw needn't show every extreme that they name: `doc_ids`: document numbers never fall along the prompt; every one of them occurs, on 1 to 6144 consecutive positions, and one document is exactly 6144 long.
All inputs are finite; a program needn't handle non-finite values.
Results may differ from the reference program's by a relative error of at most 0.019.
Values may be sent and summed in bfloat16 or wider, within the bound.
A program may use at most 64 MiB of HBM per device.

```python
import math
import jax
import jax.numpy as jnp
import numpy as np
from jax import lax

D = 5120
QUERY_HEADS = 40
KEY_VALUE_HEADS = 8
HEAD_WIDTH = 128
DOCS = 6
PROMPT_TOKENS = 12288


def starting_rows(key, width):
    first = jax.random.fold_in(key, 0)
    normal_part = jnp.clip(jax.random.normal(first, (PROMPT_TOKENS, width), jnp.float32), -4.5, 4.5)
    return normal_part


def shared_keys(key):
    base_offset = starting_rows(jax.random.fold_in(key, 7), KEY_VALUE_HEADS * HEAD_WIDTH)
    return base_offset


def draw_keys(key, part):
    result = shared_keys(key)
    return result.astype(jnp.bfloat16)


def draw_queries(key, part):
    own = jax.random.fold_in(key, 3)
    result = starting_rows(own, QUERY_HEADS * HEAD_WIDTH)
    return result.astype(jnp.bfloat16)


def block_levels(own_key, shape, cuts, smallest, high):
    loudness, own = 1.0, jax.random.fold_in(own_key, 6)
    for axis_at, shards_of in cuts:
        steps = jnp.exp(jax.random.uniform(jax.random.fold_in(own, axis_at), (shards_of,), jnp.float32, smallest / len(cuts), high / len(cuts)))
        loudness = loudness * jnp.repeat(steps, shape[axis_at] // shards_of).reshape([-1 if axis == axis_at else 1 for axis in range(len(shape))])
    return loudness


def split_up(amount, total, limit, lean):
    loads = [(1 << 20) // math.isqrt(grade ** lean) + 1 for grade in range(2, amount + 1)]
    spare, counts = total - limit - (amount - 1), [1] * (amount - 1)
    while spare > 0:
        candidates = [i for i in range(amount - 1) if counts[i] < limit]
        pool, remaining = sum([loads[i] for i in candidates]), spare
        for i in candidates:
            more = min(limit - counts[i], max(1, remaining * loads[i] // pool), spare)
            counts[i] = counts[i] + more
            spare = spare - more
    return np.array([limit] + counts)


def ragged(key, amount, total, reach, slope):
    if amount == 2:
        one = jax.random.randint(key, (), max(1, total - reach), min(reach, total - 1) + 1)
        return jnp.stack([one, total - one])
    sizes = jnp.asarray(split_up(amount, total, reach, slope), jnp.int32)
    couples = (amount - 1) // 2
    giver, sink = sizes[1:1 + 2 * couples:2], sizes[2:2 + 2 * couples:2]
    room = jnp.minimum(giver - 1, reach - sink)
    passed = jax.random.randint(jax.random.fold_in(key, 1), (couples,), 0, 1 << 20) % (room + 1)
    sizes = sizes.at[1:1 + 2 * couples:2].set(giver - passed).at[2:2 + 2 * couples:2].set(sink + passed)
    return sizes[jax.random.permutation(jax.random.fold_in(key, 2), amount)]


def bell_draw(key, extent, deviation, bound, cuts=(), kind=jnp.bfloat16):
    values = jax.random.normal(key, extent, jnp.float32) * deviation
    if len(cuts) > 0:
        values = block_levels(key, extent, cuts, -0.22, 0.18) * values
    return jnp.clip(values, min=-bound, max=bound).astype(kind)


def setup_inputs(seed: int = 0) -> dict:
    key_list = jax.random.split(jax.random.key(seed), 6)
    queries = draw_queries(jax.random.fold_in(key_list[5], 71), 0)
    keys = draw_keys(jax.random.fold_in(key_list[5], 71), 0)
    values = bell_draw(key_list[2], (PROMPT_TOKENS, KEY_VALUE_HEADS * HEAD_WIDTH), 1.0, 6.0, ((0, 64), (1, 8)))
    doc_ids = jnp.searchsorted(jnp.cumsum(ragged(key_list[3], DOCS, PROMPT_TOKENS, PROMPT_TOKENS // 2, 0)), jnp.arange(PROMPT_TOKENS), side="right").astype(jnp.int32)
    w_out = bell_draw(key_list[4], (QUERY_HEADS * HEAD_WIDTH, D), (QUERY_HEADS * HEAD_WIDTH) ** -0.5, 0.078125, ((0, 8), (1, 64)))
    return {"queries": queries, "keys": keys, "values": values, "doc_ids": doc_ids, "w_out": w_out}


def reference(queries, keys, values, doc_ids, w_out):
    group_width = QUERY_HEADS // KEY_VALUE_HEADS
    scale = 1.0 / math.sqrt(HEAD_WIDTH)
    block = math.gcd(PROMPT_TOKENS, 512)
    q_heads = queries.reshape(PROMPT_TOKENS, QUERY_HEADS, HEAD_WIDTH).transpose(1, 0, 2)
    key_head_rows = keys.reshape(PROMPT_TOKENS, KEY_VALUE_HEADS, HEAD_WIDTH).transpose(1, 0, 2)
    value_head_rows = values.reshape(PROMPT_TOKENS, KEY_VALUE_HEADS, HEAD_WIDTH).transpose(1, 0, 2).astype(jnp.float32)
    positions = jnp.arange(PROMPT_TOKENS, dtype=jnp.int32)

    def one_block(index):
        start = (index * block).astype(jnp.int32)
        q_pos = start + jnp.arange(block, dtype=jnp.int32)
        q_doc = lax.dynamic_slice_in_dim(doc_ids, start, block, 0)
        visible = (doc_ids[None, :] == q_doc[:, None]) & (positions[None, :] <= q_pos[:, None])
        q_block = lax.dynamic_slice_in_dim(q_heads, start, block, 1)

        def one_head(head):
            query = lax.dynamic_index_in_dim(q_block, head, 0, False)
            key_head = lax.dynamic_index_in_dim(key_head_rows, head // group_width, 0, False)
            value_head = lax.dynamic_index_in_dim(value_head_rows, head // group_width, 0, False)
            scores = jnp.dot(query, key_head.T, preferred_element_type=jnp.float32) * scale
            masked = jnp.where(visible, scores, -jnp.inf)
            top = lax.optimization_barrier(jnp.max(masked, axis=1, keepdims=True))
            weights = jnp.where(visible, jnp.exp(masked - top), 0.0)
            total = lax.optimization_barrier(jnp.sum(weights, axis=1, keepdims=True))
            summed = jnp.dot(weights, value_head, precision=lax.Precision.HIGHEST)
            return summed / total
        return lax.map(one_head, jnp.arange(QUERY_HEADS, dtype=jnp.int32))
    blocks = lax.map(one_block, jnp.arange(PROMPT_TOKENS // block, dtype=jnp.int32))
    attended = blocks.transpose(0, 2, 1, 3).reshape(PROMPT_TOKENS, QUERY_HEADS * HEAD_WIDTH).astype(jnp.bfloat16)
    return jnp.dot(attended, w_out, preferred_element_type=jnp.float32).astype(jnp.bfloat16)
```

```python
import functools
import math

import jax
import jax.numpy as jnp
from jax import lax
from jax.experimental import pallas as pl
from jax.experimental.pallas import tpu as pltpu
from jax.sharding import PartitionSpec as P

MESH = pl.DeviceIdType.MESH
F32, BF16 = jnp.float32, jnp.bfloat16
NT = (((1,), (1,)), ((), ()))

NZ, NX, NY = 8, 4, 8
T = 192
HEADS = 5
W = 128
STAT = 16
KVR = T + STAT
DEPTH = 5
COLS = 80
K = HEADS * W
GROUP = 48
PACK = T + GROUP
SCALE = math.log2(math.e) / math.sqrt(W)
HIDE = -131072.0


def dot_nt(a, b):
    return lax.dot_general(a, b, NT, preferred_element_type=F32)


def split_of(j):
    return 128 if j < 2 else 112


def kernel(q_ref, k_ref, v_ref, d_ref, w_ref, o_ref,
           kv, ff, qa, acc, top, wz, wr, ag, sbuf, rbuf, fsend, fin, selm, selr,
           kvz_s, kvz_r, kvx_s, kvx_r, kvd_s, kvd_r, wz_s, wz_r, wd_s, wd_r,
           ax_s, ax_r, rs_s, rs_r, fx_s, fx_r):
    s = lax.axis_index("seq")
    t = lax.axis_index("tp")
    z, x, c = s // 8, lax.rem(s // 2, 4), lax.rem(s, 2)
    me = x * 2 + c

    def dev(dz=0, dx=0, dc=0, dy=0):
        zz = lax.rem(z + dz + NZ, NZ)
        xx = lax.rem(x + dx + NX, NX)
        cc = lax.rem(c + dc, 2)
        return (zz * 8 + xx * 2 + cc, lax.rem(t + dy + NY, NY))

    up, down = dev(dz=1), dev(dz=-1)
    right, left = dev(dx=1), dev(dx=-1)
    sib = dev(dc=1)
    xr, xl, xo = lax.rem(x + 1, NX), lax.rem(x + 3, NX), lax.rem(x + 2, NX)
    oc = 1 - c

    def rc(ref, ss, rs, to):
        return pltpu.make_async_remote_copy(
            src_ref=ref, dst_ref=ref, send_sem=ss, recv_sem=rs, device_id=to, device_id_type=MESH)

    barrier = pltpu.get_barrier_semaphore()
    peers = [up, down, right, left, dev(dx=2), sib, dev(dy=1), dev(dy=-1)]
    for peer in peers:
        pl.semaphore_signal(barrier, inc=1, device_id=peer, device_id_type=MESH)

    kv[0, c, x, 0:T, 0:W] = k_ref[...]
    kv[0, c, x, 0:T, W:2 * W] = v_ref[...]
    docs = jnp.broadcast_to(d_ref[...], (W, T))
    number = lax.broadcasted_iota(jnp.int32, (W, T), 0)
    first = jnp.sum((docs < number).astype(F32), axis=1, keepdims=True)
    last = jnp.sum((docs <= number).astype(F32), axis=1, keepdims=True)
    first = jnp.transpose(jnp.broadcast_to(first, (W, W)))
    last = jnp.transpose(jnp.broadcast_to(last, (W, W)))
    stat = jnp.concatenate([first[0:8], last[0:8]], axis=0).astype(BF16)
    kv[0, c, x, T:KVR, 0:W] = stat
    kv[0, c, x, T:KVR, W:2 * W] = jnp.zeros((STAT, W), BF16)
    wz[z, c] = w_ref[...]

    pl.semaphore_wait(barrier, len(peers))

    started = []

    def go(copy):
        copy.start()
        started.append(copy)

    def x_start(p):
        blk = kv.at[p, c, x]
        go(rc(blk, kvx_s.at[p, 0], kvx_r.at[p, 0], right))
        go(rc(blk, kvx_s.at[p, 1], kvx_r.at[p, 1], left))
        go(rc(blk, kvd_s.at[p, 0], kvd_r.at[p, 0], sib))

    def x_relay(p):
        rc(kv.at[p, c, xl], kvx_s.at[p, 0], kvx_r.at[p, 0], right).wait_recv()
        go(rc(kv.at[p, c, xl, pl.ds(0, 96)], kvx_s.at[p, 2], kvx_r.at[p, 2], right))
        go(rc(kv.at[p, c, xl], kvd_s.at[p, 1], kvd_r.at[p, 1], sib))
        rc(kv.at[p, c, xr], kvx_s.at[p, 1], kvx_r.at[p, 1], left).wait_recv()
        go(rc(kv.at[p, c, xr, pl.ds(96, 112)], kvx_s.at[p, 3], kvx_r.at[p, 3], left))
        go(rc(kv.at[p, c, xr], kvd_s.at[p, 2], kvd_r.at[p, 2], sib))

    def x_end(p):
        rc(kv.at[p, c, xo, pl.ds(0, 96)], kvx_s.at[p, 2], kvx_r.at[p, 2], right).wait_recv()
        rc(kv.at[p, c, xo, pl.ds(96, 112)], kvx_s.at[p, 3], kvx_r.at[p, 3], left).wait_recv()
        go(rc(kv.at[p, c, xo], kvd_s.at[p, 3], kvd_r.at[p, 3], sib))

    def sib_wait(p):
        for i, xx in enumerate((x, xl, xr, xo)):
            rc(kv.at[p, oc, xx], kvd_s.at[p, i], kvd_r.at[p, i], sib).wait_recv()

    def z_send(p):
        return pltpu.make_async_remote_copy(
            src_ref=kv.at[p, c, x], dst_ref=kv.at[p + 1, c, x], send_sem=kvz_s.at[p], recv_sem=kvz_r.at[p],
            device_id=up, device_id_type=MESH)

    def z_step(p):
        z_send(p - 1).wait_recv()
        if p < DEPTH - 1:
            go(z_send(p))
        x_start(p)

    def w_down(i):
        return rc(wz.at[lax.rem(z + i, NZ), c], wz_s.at[i], wz_r.at[i], down)

    def w_up(i):
        return rc(wz.at[lax.rem(z - i + NZ, NZ), c], wz_s.at[4 + i], wz_r.at[4 + i], up)

    def w_sib(plane, i):
        return rc(wz.at[plane, c], wd_s.at[i], wd_r.at[i], sib)

    def w_down_step(i):
        plane = lax.rem(z + i, NZ)
        rc(wz.at[plane, c], wz_s.at[i - 1], wz_r.at[i - 1], down).wait_recv()
        if i < 4:
            go(w_down(i))
        go(w_sib(plane, i))

    def w_up_step(i):
        plane = lax.rem(z - i + NZ, NZ)
        rc(wz.at[plane, c], wz_s.at[3 + i], wz_r.at[3 + i], up).wait_recv()
        if i < 3:
            go(w_up(i))
        go(w_sib(plane, 4 + i))

    go(z_send(0))
    x_start(0)
    go(w_down(0))
    go(w_sib(z, 0))

    row = lax.broadcasted_iota(jnp.int32, (T, W), 0).astype(F32)

    def doc_rows(bounds):
        bounds = bounds.astype(F32)
        return jnp.where((row >= bounds[0:1]) & (row < bounds[8:9]), 1.0, 0.0)

    own_docs = doc_rows(stat)
    feature = jnp.where(own_docs > 0.5, 0.0, HIDE).astype(BF16)
    for h in range(HEADS):
        qa[h * T:(h + 1) * T, 0:W] = q_ref[:, h * W:(h + 1) * W]
        qa[h * T:(h + 1) * T, W:2 * W] = feature
    k_own = jnp.concatenate([k_ref[...], own_docs.astype(BF16)], axis=1)
    v_own = jnp.concatenate([v_ref[...], jnp.ones((T, W), BF16)], axis=1)
    causal = lax.broadcasted_iota(jnp.int32, (T, T), 0) >= lax.broadcasted_iota(jnp.int32, (T, T), 1)
    for h in range(HEADS):
        rows = slice(h * T, (h + 1) * T)
        scores = jnp.where(causal, dot_nt(qa[rows, :], k_own), -1e30)
        high = jnp.broadcast_to(jnp.max(scores, axis=1, keepdims=True) * SCALE, (T, W))
        weights = jnp.exp2(scores * SCALE - high[:, 0:1]).astype(BF16)
        top[rows, :] = high
        acc[rows, :] = jnp.dot(weights, v_own, preferred_element_type=F32)

    r5 = lax.broadcasted_iota(jnp.int32, (NX * W, K), 0)
    col = lax.broadcasted_iota(jnp.int32, (NX * W, K), 1)
    part, lane = r5 // W, lax.rem(r5, W)
    selm[...] = jnp.where(col == part * 160 + lane + jnp.where(lane < 64, 0, 16), 1.0, 0.0).astype(BF16)
    spot = lax.rem(lane, 32)
    goal = part * 160 + spot + jnp.where(spot < 16, 64, 128)
    for g in range(4):
        selr[g] = jnp.where((col == goal) & (lane // 32 == g), 1.0, 0.0).astype(BF16)
    wr[...] = jnp.zeros_like(wr)

    def attend(blocks, valid):
        for b in range(8):
            docs_b = doc_rows(kv[blocks[b], b // 4, b % 4, T:KVR, 0:W])
            ff[b] = jnp.where(valid[b], docs_b, 1.0).astype(BF16)
        half = HEADS * T // 2
        for u in range(2):
            rows = slice(u * half, (u + 1) * half)
            keys = jnp.concatenate([kv[blocks[b], b // 4, b % 4, 0:T, 0:W] for b in range(8)], axis=0)
            keys = jnp.concatenate([keys, ff[...].reshape(8 * T, W)], axis=1)
            scores = dot_nt(qa[rows, :], keys)
            old = top[rows, :]
            new = jnp.maximum(old, jnp.max(scores, axis=1, keepdims=True) * SCALE)
            weights = jnp.exp2(scores * SCALE - new[:, 0:1]).astype(BF16)
            vals = jnp.concatenate([kv[blocks[b], b // 4, b % 4, 0:T, W:2 * W] for b in range(8)], axis=0)
            vals = jnp.concatenate([vals, jnp.ones((8 * T, W), BF16)], axis=1)
            keep = jnp.exp2(old - new)
            acc[rows, :] = acc[rows, :] * jnp.concatenate([keep, keep], axis=1) + jnp.dot(
                weights, vals, preferred_element_type=F32)
            top[rows, :] = new

    def attend_plane(p):
        sib_wait(p)
        attend([p] * 8, [z >= p] * 8)

    z_step(1)
    x_relay(0)
    w_down_step(1)
    z_step(2)
    x_end(0)
    x_relay(1)
    z_step(3)
    x_end(1)
    attend_plane(1)
    z_step(4)
    go(w_up(0))
    x_relay(2)
    x_end(2)
    w_down_step(2)
    attend_plane(2)
    x_relay(3)
    w_down_step(3)
    w_up_step(1)
    x_end(3)
    attend_plane(3)
    x_relay(4)
    x_end(4)
    w_up_step(2)
    w_down_step(4)
    sib_wait(0)
    sib_wait(4)
    early = [(b % 4) * 2 + b // 4 < me for b in range(8)]
    attend([jnp.where(e, 0, 4) for e in early], [e | (z >= 4) for e in early])
    w_up_step(3)

    for h in range(HEADS):
        rows = slice(h * T, (h + 1) * T)
        ag[x, :, h * W:(h + 1) * W] = (acc[rows, 0:W] / acc[rows, W:2 * W]).astype(BF16)
    go(rc(ag.at[x], ax_s.at[0], ax_r.at[0], right))
    go(rc(ag.at[x], ax_s.at[1], ax_r.at[1], left))

    for i in range(NZ):
        plane = lax.rem(z + i, NZ) if i <= 4 else lax.rem(z - (i - 4) + NZ, NZ)
        rc(wz.at[plane, oc], wd_s.at[i], wd_r.at[i], sib).wait_recv()
    for o in range(NY):
        wr[o, 96:112, :] = wz[o, 0, 64:80, :]
        wr[o, 112:128, :] = wz[o, 1, 64:80, :]

    def main_cols(o):
        return jnp.concatenate([wz[o, 0, 0:64, :], wz[o, 1, 0:64, :]], axis=0)

    def part_up(j, o):
        return dot_nt(ag[lax.rem(x + j, NX), 0:split_of(j), :], main_cols(o))

    def part_down(j, o):
        xx = lax.rem(x + j, NX)
        main = dot_nt(ag[xx, split_of(j):T, :], main_cols(o))
        rest = dot_nt(ag[xx, 0:GROUP, :], wr[o, 96:224, :])
        for g in range(1, 4):
            rest += dot_nt(ag[xx, g * GROUP:(g + 1) * GROUP, :], wr[o, 96 - 32 * g:224 - 32 * g, :])
        return jnp.concatenate([main, rest], axis=0)

    y_up, y_down = dev(dy=1), dev(dy=-1)

    def rs(d, k, j):
        n = split_of(j) if d == 0 else PACK - split_of(j)
        return pltpu.make_async_remote_copy(
            src_ref=sbuf.at[d, k, j, pl.ds(0, n)], dst_ref=rbuf.at[d, k, j, pl.ds(0, n)],
            send_sem=rs_s.at[d, k, j], recv_sem=rs_r.at[d, k, j],
            device_id=y_up if d == 0 else y_down, device_id_type=MESH)

    def step(d, k, j, first_step):
        o = lax.rem(t + 7 - k, NY) if d == 0 else lax.rem(t + 1 + k, NY)
        n = split_of(j) if d == 0 else PACK - split_of(j)
        total = part_up(j, o) if d == 0 else part_down(j, o)
        if not first_step:
            rs(d, k - 1, j).wait_recv()
            total = total + rbuf[d, k - 1, j, 0:n, :].astype(F32)
        return total

    def send_step(k, first_step):
        for j in range(NX):
            if first_step and j == 1:
                rc(ag.at[xr], ax_s.at[1], ax_r.at[1], left).wait_recv()
                go(rc(ag.at[xr, pl.ds(96, 96)], ax_s.at[3], ax_r.at[3], left))
                rc(ag.at[xl], ax_s.at[0], ax_r.at[0], right).wait_recv()
                go(rc(ag.at[xl, pl.ds(0, 96)], ax_s.at[2], ax_r.at[2], right))
            if first_step and j == 2:
                rc(ag.at[xo, pl.ds(0, 96)], ax_s.at[2], ax_r.at[2], right).wait_recv()
                rc(ag.at[xo, pl.ds(96, 96)], ax_s.at[3], ax_r.at[3], left).wait_recv()
            for d in range(2):
                n = split_of(j) if d == 0 else PACK - split_of(j)
                sbuf[d, k, j, 0:n, :] = step(d, k, j, first_step).astype(BF16)
                rs(d, k, j).start()

    send_step(0, True)

    def loop(k, carry):
        send_step(k, False)
        return carry

    lax.fori_loop(1, 7, loop, 0)

    def fx(j):
        to = lax.rem(x + j, NX)
        return pltpu.make_async_remote_copy(
            src_ref=fsend.at[j - 1], dst_ref=fin.at[x], send_sem=fx_s.at[j - 1], recv_sem=fx_r.at[j - 1],
            device_id=(z * 8 + to * 2 + c, t), device_id_type=MESH)

    for j in (1, 2, 3, 0):
        block = jnp.concatenate([step(0, 7, j, False), step(1, 7, j, False)], axis=0).astype(BF16)
        if j == 0:
            fin[x] = block
        else:
            fsend[j - 1] = block
            go(fx(j))
    for j in (1, 2, 3):
        pltpu.make_async_remote_copy(
            src_ref=fsend.at[j - 1], dst_ref=fin.at[lax.rem(x - j + NX, NX)], send_sem=fx_s.at[j - 1],
            recv_sem=fx_r.at[j - 1], device_id=dev(dx=j), device_id_type=MESH).wait_recv()

    main = jnp.concatenate([fin[i, 0:T, :] for i in range(NX)], axis=1)
    rest = jnp.concatenate([fin[i, T:PACK, :] for i in range(NX)], axis=1)
    for g in range(4):
        rows = slice(g * GROUP, (g + 1) * GROUP)
        o_ref[rows, :] = (
            jnp.dot(main[rows, :], selm[...], preferred_element_type=F32)
            + jnp.dot(rest, selr[g], preferred_element_type=F32)).astype(BF16)

    for copy in started:
        copy.wait_send()

    def drain(k, carry):
        for j in range(NX):
            for d in range(2):
                rs(d, k, j).wait_send()
        return carry

    lax.fori_loop(0, 7, drain, 0)


def local(queries, keys, values, doc_ids, w_out):
    sem = pltpu.SemaphoreType.DMA
    vmem = pl.BlockSpec(memory_space=pltpu.VMEM)
    return pl.pallas_call(
        kernel,
        out_shape=jax.ShapeDtypeStruct((T, K), BF16),
        in_specs=[vmem] * 5,
        out_specs=vmem,
        scratch_shapes=[
            pltpu.VMEM((DEPTH, 2, NX, KVR, 2 * W), BF16),
            pltpu.VMEM((8, T, W), BF16),
            pltpu.VMEM((HEADS * T, 2 * W), BF16),
            pltpu.VMEM((HEADS * T, 2 * W), F32),
            pltpu.VMEM((HEADS * T, W), F32),
            pltpu.VMEM((NZ, 2, COLS, K), BF16),
            pltpu.VMEM((NY, 224, K), BF16),
            pltpu.VMEM((NX, T, K), BF16),
            pltpu.VMEM((2, 7, NX, 128, W), BF16),
            pltpu.VMEM((2, 7, NX, 128, W), BF16),
            pltpu.VMEM((3, PACK, W), BF16),
            pltpu.VMEM((NX, PACK, W), BF16),
            pltpu.VMEM((NX * W, K), BF16),
            pltpu.VMEM((4, NX * W, K), BF16),
            sem((4,)), sem((4,)), sem((5, 4)), sem((5, 4)), sem((5, 4)), sem((5, 4)),
            sem((7,)), sem((7,)), sem((8,)), sem((8,)),
            sem((4,)), sem((4,)), sem((2, 7, NX)), sem((2, 7, NX)), sem((3,)), sem((3,)),
        ],
        compiler_params=pltpu.CompilerParams(
            collective_id=0, has_side_effects=True, vmem_limit_bytes=56 * 2**20),
        name="attend_project",
    )(queries, keys, values, doc_ids.reshape(1, T), w_out.T)


def solution(mesh):
    placed = (P("seq", "tp"), P("seq", "tp"), P("seq", "tp"), P("seq"), P("tp", "seq"))
    return jax.shard_map(
        local, mesh=mesh, in_specs=placed, out_specs=P("seq", "tp"), check_vma=False
    )
```

```python
import functools
import math

import jax
import jax.numpy as jnp
from jax import lax
from jax.experimental import pallas as pl
from jax.experimental.pallas import tpu as pltpu
from jax.sharding import PartitionSpec as P

MESH = pl.DeviceIdType.MESH
F32, BF16 = jnp.float32, jnp.bfloat16
NT = (((1,), (1,)), ((), ()))

NZ, NX, NY = 8, 4, 8
T = 192
HEADS = 5
W = 128
STAT = 16
KVR = T + STAT
DEPTH = 5
COLS = 80
K = HEADS * W
GROUP = 48
PACK = T + GROUP
SCALE = math.log2(math.e) / math.sqrt(W)
HIDE = -131072.0


def dot_nt(a, b):
    return lax.dot_general(a, b, NT, preferred_element_type=F32)


def kernel(q_hbm, k_hbm, v_hbm, d_hbm, w_hbm, o_ref,
           kv, ff, qv, dv, qa, acc, top, wz, wr, ag, sbuf, rbuf, fsend, fin, selm, selr,
           in_s, kvz_s, kvz_r, kvx_s, kvx_r, kvd_s, kvd_r, wz_s, wz_r, wd_s, wd_r,
           ax_s, ax_r, rs_s, rs_r, fx_s, fx_r):
    s = lax.axis_index("seq")
    t = lax.axis_index("tp")
    z, x, c = s // 8, lax.rem(s // 2, 4), lax.rem(s, 2)
    me = x * 2 + c

    def dev(dz=0, dx=0, dc=0, dy=0):
        zz = lax.rem(z + dz + NZ, NZ)
        xx = lax.rem(x + dx + NX, NX)
        cc = lax.rem(c + dc, 2)
        return (zz * 8 + xx * 2 + cc, lax.rem(t + dy + NY, NY))

    up, right, left, across = dev(dz=1), dev(dx=1), dev(dx=-1), dev(dx=2)
    sib = dev(dc=1)
    xr, xl, xo = lax.rem(x + 1, NX), lax.rem(x + 3, NX), lax.rem(x + 2, NX)
    oc = 1 - c

    def rc(ref, ss, rs, to):
        return pltpu.make_async_remote_copy(
            src_ref=ref, dst_ref=ref, send_sem=ss, recv_sem=rs, device_id=to, device_id_type=MESH)

    barrier = pltpu.get_barrier_semaphore()
    peers = [dev(dz=i) for i in range(1, NZ)] + [right, left, across, sib, dev(dy=1), dev(dy=-1)]
    for peer in peers:
        pl.semaphore_signal(barrier, inc=1, device_id=peer, device_id_type=MESH)
    loads = [
        pltpu.make_async_copy(d_hbm, dv, in_s.at[0]),
        pltpu.make_async_copy(k_hbm, kv.at[0, c, x, pl.ds(0, T), pl.ds(0, W)], in_s.at[1]),
        pltpu.make_async_copy(v_hbm, kv.at[0, c, x, pl.ds(0, T), pl.ds(W, W)], in_s.at[2]),
        pltpu.make_async_copy(w_hbm, wz.at[z, c], in_s.at[3]),
        pltpu.make_async_copy(q_hbm, qv, in_s.at[4]),
    ]
    for load in loads:
        load.start()

    loads[0].wait()
    docs = jnp.broadcast_to(dv[...], (W, T))
    number = lax.broadcasted_iota(jnp.int32, (W, T), 0)
    first = jnp.sum((docs < number).astype(F32), axis=1, keepdims=True)
    last = jnp.sum((docs <= number).astype(F32), axis=1, keepdims=True)
    first = jnp.transpose(jnp.broadcast_to(first, (W, W)))
    last = jnp.transpose(jnp.broadcast_to(last, (W, W)))
    stat = jnp.concatenate([first[0:8], last[0:8]], axis=0).astype(BF16)
    kv[0, c, x, T:KVR, 0:W] = stat
    kv[0, c, x, T:KVR, W:2 * W] = jnp.zeros((STAT, W), BF16)
    loads[1].wait()
    loads[2].wait()

    pl.semaphore_wait(barrier, len(peers))

    started = []

    def go(copy):
        copy.start()
        started.append((copy, None))

    def go_if(cond, copy):
        @pl.when(cond)
        def _():
            copy.start()
        started.append((copy, cond))

    def z_copy(p, half):
        rows = pl.ds(0, 96) if half == 0 else pl.ds(96, KVR - 96)
        return pltpu.make_async_remote_copy(
            src_ref=kv.at[p, c, x, rows], dst_ref=kv.at[p + 1, c, x, rows], send_sem=kvz_s.at[p, half],
            recv_sem=kvz_r.at[p, half], device_id=up, device_id_type=MESH)

    def x_start(p):
        blk = kv.at[p, c, x]
        go(rc(blk, kvx_s.at[p, 0], kvx_r.at[p, 0], right))
        go(rc(blk, kvx_s.at[p, 1], kvx_r.at[p, 1], left))
        go(rc(blk, kvx_s.at[p, 2], kvx_r.at[p, 2], across))
        go(rc(blk, kvd_s.at[p, 0], kvd_r.at[p, 0], sib))

    def side(dest):
        return jnp.where(x < dest, 0, 4)

    def x_start_mixed(p):
        for i, (to, dest) in enumerate(((right, xr), (left, xl), (across, xo))):
            blk = kv.at[p, c, x]
            go_if((x < dest) if p == 0 else (x > dest), rc(blk, kvx_s.at[p, i], kvx_r.at[0, i], to))
        go_if(c == (0 if p == 0 else 1), rc(kv.at[p, c, x], kvd_s.at[p, 0], kvd_r.at[0, 0], sib))

    def plane_of(p, xx):
        return p if p > 0 else jnp.where(xx < x, 0, 4)

    def x_end(p):
        for i, xx in enumerate((xl, xr, xo)):
            ref = kv.at[plane_of(p, xx), c, xx]
            rc(ref, kvx_s.at[p, i], kvx_r.at[p, i], right).wait_recv()
            go(rc(ref, kvd_s.at[p, i + 1], kvd_r.at[p, i + 1], sib))

    def sib_wait(p):
        own = p if p > 0 else jnp.where(c == 1, 0, 4)
        for i, (pp, xx) in enumerate(((own, x), (plane_of(p, xl), xl), (plane_of(p, xr), xr), (plane_of(p, xo), xo))):
            rc(kv.at[pp, oc, xx], kvd_s.at[p, i], kvd_r.at[p, i], sib).wait_recv()

    def z_step(p):
        for half in range(2):
            z_copy(p - 1, half).wait_recv()
            if p < DEPTH - 1:
                go(z_copy(p, half))
        if p < DEPTH - 1:
            x_start(p)
        else:
            x_start_mixed(p)

    def w_send(i):
        go(rc(wz.at[z, c], wz_s.at[i], wz_r.at[i], dev(dz=-i)))

    def w_recv(i):
        ref = wz.at[lax.rem(z + i, NZ), c]
        rc(ref, wz_s.at[i], wz_r.at[i], up).wait_recv()
        go(rc(ref, wd_s.at[i], wd_r.at[i], sib))

    go(z_copy(0, 0))
    go(z_copy(0, 1))
    x_start_mixed(0)
    loads[3].wait()
    for i in (1, 2, 3, 4):
        w_send(i)
    go(rc(wz.at[z, c], wd_s.at[0], wd_r.at[0], sib))

    row = lax.broadcasted_iota(jnp.int32, (T, W), 0).astype(F32)

    def doc_rows(bounds):
        bounds = bounds.astype(F32)
        return jnp.where((row >= bounds[0:1]) & (row < bounds[8:9]), 1.0, 0.0)

    own_docs = doc_rows(stat)
    feature = jnp.where(own_docs > 0.5, 0.0, HIDE).astype(BF16)
    loads[4].wait()
    for h in range(HEADS):
        qa[h * T:(h + 1) * T, 0:W] = qv[:, h * W:(h + 1) * W]
        qa[h * T:(h + 1) * T, W:2 * W] = feature
    k_own = jnp.concatenate([kv[0, c, x, 0:T, 0:W], own_docs.astype(BF16)], axis=1)
    v_own = jnp.concatenate([kv[0, c, x, 0:T, W:2 * W], jnp.ones((T, W), BF16)], axis=1)
    causal = lax.broadcasted_iota(jnp.int32, (T, T), 0) >= lax.broadcasted_iota(jnp.int32, (T, T), 1)

    def diagonal(h):
        rows = slice(h * T, (h + 1) * T)
        scores = jnp.where(causal, dot_nt(qa[rows, :], k_own), -1e30)
        high = jnp.broadcast_to(jnp.max(scores, axis=1, keepdims=True) * SCALE, (T, W))
        weights = jnp.exp2(scores * SCALE - high[:, 0:1]).astype(BF16)
        top[rows, :] = high
        acc[rows, :] = jnp.dot(weights, v_own, preferred_element_type=F32)

    def attend(blocks, valid):
        for b in range(8):
            docs_b = doc_rows(kv[blocks[b], b // 4, b % 4, T:KVR, 0:W])
            ff[b] = jnp.where(valid[b], docs_b, 1.0).astype(BF16)
        half = HEADS * T // 2
        for u in range(2):
            rows = slice(u * half, (u + 1) * half)
            keys = jnp.concatenate([kv[blocks[b], b // 4, b % 4, 0:T, 0:W] for b in range(8)], axis=0)
            keys = jnp.concatenate([keys, ff[...].reshape(8 * T, W)], axis=1)
            scores = dot_nt(qa[rows, :], keys)
            old = top[rows, :]
            new = jnp.maximum(old, jnp.max(scores, axis=1, keepdims=True) * SCALE)
            weights = jnp.exp2(scores * SCALE - new[:, 0:1]).astype(BF16)
            vals = jnp.concatenate([kv[blocks[b], b // 4, b % 4, 0:T, W:2 * W] for b in range(8)], axis=0)
            vals = jnp.concatenate([vals, jnp.ones((8 * T, W), BF16)], axis=1)
            keep = jnp.exp2(old - new)
            acc[rows, :] = acc[rows, :] * jnp.concatenate([keep, keep], axis=1) + jnp.dot(
                weights, vals, preferred_element_type=F32)
            top[rows, :] = new

    def attend_plane(p):
        sib_wait(p)
        attend([p] * 8, [z >= p] * 8)

    z_step(1)
    diagonal(0)
    diagonal(1)
    z_step(2)
    x_end(1)
    diagonal(2)
    diagonal(3)
    z_step(3)
    diagonal(4)
    z_step(4)
    for i in (5, 6, 7):
        w_send(i)
    x_end(2)
    attend_plane(1)
    x_end(3)
    attend_plane(2)
    x_end(0)
    attend_plane(3)
    for i in (1, 2, 3):
        w_recv(i)
    sib_wait(0)
    early = [(b % 4) * 2 + b // 4 < me for b in range(8)]
    attend([jnp.where(e, 0, 4) for e in early], [e | (z >= 4) for e in early])

    for h in range(HEADS):
        rows = slice(h * T, (h + 1) * T)
        ag[x, :, h * W:(h + 1) * W] = (acc[rows, 0:W] / acc[rows, W:2 * W]).astype(BF16)
    lo, hi = pl.ds(0, 96), pl.ds(96, 96)
    go(rc(ag.at[x, lo], ax_s.at[0], ax_r.at[0], right))
    go(rc(ag.at[x, hi], ax_s.at[2], ax_r.at[2], left))
    go(rc(ag.at[x, hi], ax_s.at[1], ax_r.at[1], right))
    go(rc(ag.at[x, lo], ax_s.at[3], ax_r.at[3], left))

    for i in (5, 6, 7, 4):
        w_recv(i)
    wr[...] = jnp.zeros_like(wr)
    for i in range(NZ):
        plane = lax.rem(z + i, NZ)
        rc(wz.at[plane, oc], wd_s.at[i], wd_r.at[i], sib).wait_recv()
    for o in range(NY):
        wr[o, 96:112, :] = wz[o, 0, 64:80, :]
        wr[o, 112:128, :] = wz[o, 1, 64:80, :]

    def partial(j, o):
        xx = lax.rem(x + j, NX)
        cols = jnp.concatenate([wz[o, 0, 0:64, :], wz[o, 1, 0:64, :]], axis=0)
        main = dot_nt(ag[xx], cols)
        rest = dot_nt(ag[xx, 0:GROUP, :], wr[o, 96:224, :])
        for g in range(1, 4):
            rest += dot_nt(ag[xx, g * GROUP:(g + 1) * GROUP, :], wr[o, 96 - 32 * g:224 - 32 * g, :])
        return jnp.concatenate([main, rest], axis=0)

    y_up, y_down = dev(dy=1), dev(dy=-1)

    def hops(d, j):
        return 4 if (d + j) % 2 == 1 else 3

    def rs(d, r, j):
        return pltpu.make_async_remote_copy(
            src_ref=sbuf.at[d, r - 1, j], dst_ref=rbuf.at[d, r - 1, j],
            send_sem=rs_s.at[d, r - 1, j], recv_sem=rs_r.at[d, r - 1, j],
            device_id=y_up if d == 0 else y_down, device_id_type=MESH)

    def send_step(n, j):
        for d in range(2):
            r = hops(d, j) - n
            if r < 1:
                continue
            o = lax.rem(t + r, NY) if d == 0 else lax.rem(t - r + NY, NY)
            total = partial(j, o)
            if n > 0:
                rs(d, r + 1, j).wait_recv()
                total = total + rbuf[d, r, j].astype(F32)
            sbuf[d, r - 1, j] = total.astype(BF16)
            go(rs(d, r, j))

    def fx(j):
        return pltpu.make_async_remote_copy(
            src_ref=fsend.at[j - 1], dst_ref=fin.at[x], send_sem=fx_s.at[j - 1], recv_sem=fx_r.at[j - 1],
            device_id=dev(dx=j), device_id_type=MESH)

    def finish(j):
        total = partial(j, t)
        for d in range(2):
            rs(d, 1, j).wait_recv()
            total = total + rbuf[d, 0, j].astype(F32)
        if j == 0:
            fin[x] = total.astype(BF16)
        else:
            fsend[j - 1] = total.astype(BF16)
            go(fx(j))

    send_step(0, 0)
    rc(ag.at[xl, lo], ax_s.at[0], ax_r.at[0], right).wait_recv()
    go(rc(ag.at[xl, lo], ax_s.at[4], ax_r.at[4], right))
    rc(ag.at[xr, hi], ax_s.at[2], ax_r.at[2], left).wait_recv()
    go(rc(ag.at[xr, hi], ax_s.at[5], ax_r.at[5], left))
    send_step(1, 0)

    r5 = lax.broadcasted_iota(jnp.int32, (NX * W, K), 0)
    col = lax.broadcasted_iota(jnp.int32, (NX * W, K), 1)
    part, lane = r5 // W, lax.rem(r5, W)
    selm[...] = jnp.where(col == part * 160 + lane + jnp.where(lane < 64, 0, 16), 1.0, 0.0).astype(BF16)
    spot = lax.rem(lane, 32)
    goal = part * 160 + spot + jnp.where(spot < 16, 64, 128)
    for g in range(4):
        selr[g] = jnp.where((col == goal) & (lane // 32 == g), 1.0, 0.0).astype(BF16)

    rc(ag.at[xl, hi], ax_s.at[1], ax_r.at[1], right).wait_recv()
    rc(ag.at[xr, lo], ax_s.at[3], ax_r.at[3], left).wait_recv()
    send_step(0, 1)
    send_step(0, 3)
    send_step(2, 0)
    rc(ag.at[xo, lo], ax_s.at[4], ax_r.at[4], right).wait_recv()
    rc(ag.at[xo, hi], ax_s.at[5], ax_r.at[5], left).wait_recv()
    send_step(0, 2)
    send_step(1, 1)
    send_step(1, 3)
    send_step(3, 0)
    send_step(1, 2)
    send_step(2, 1)
    send_step(2, 3)
    finish(0)
    send_step(2, 2)
    send_step(3, 1)
    send_step(3, 3)
    send_step(3, 2)
    finish(1)
    finish(3)
    finish(2)
    for j in (1, 3, 2):
        pltpu.make_async_remote_copy(
            src_ref=fsend.at[j - 1], dst_ref=fin.at[lax.rem(x - j + NX, NX)], send_sem=fx_s.at[j - 1],
            recv_sem=fx_r.at[j - 1], device_id=dev(dx=j), device_id_type=MESH).wait_recv()

    main = jnp.concatenate([fin[i, 0:T, :] for i in range(NX)], axis=1)
    rest = jnp.concatenate([fin[i, T:PACK, :] for i in range(NX)], axis=1)
    for g in range(4):
        rows = slice(g * GROUP, (g + 1) * GROUP)
        o_ref[rows, :] = (
            jnp.dot(main[rows, :], selm[...], preferred_element_type=F32)
            + jnp.dot(rest, selr[g], preferred_element_type=F32)).astype(BF16)

    for copy, cond in started:
        if cond is None:
            copy.wait_send()
        else:
            pl.when(cond)(copy.wait_send)


def local(queries, keys, values, doc_ids, w_out):
    sem = pltpu.SemaphoreType.DMA
    vmem = pl.BlockSpec(memory_space=pltpu.VMEM)
    return pl.pallas_call(
        kernel,
        out_shape=jax.ShapeDtypeStruct((T, K), BF16),
        in_specs=[pl.BlockSpec(memory_space=pl.ANY)] * 5,
        out_specs=vmem,
        scratch_shapes=[
            pltpu.VMEM((DEPTH, 2, NX, KVR, 2 * W), BF16),
            pltpu.VMEM((8, T, W), BF16),
            pltpu.VMEM((T, K), BF16),
            pltpu.VMEM((1, T), jnp.int32),
            pltpu.VMEM((HEADS * T, 2 * W), BF16),
            pltpu.VMEM((HEADS * T, 2 * W), F32),
            pltpu.VMEM((HEADS * T, W), F32),
            pltpu.VMEM((NZ, 2, COLS, K), BF16),
            pltpu.VMEM((NY, 224, K), BF16),
            pltpu.VMEM((NX, T, K), BF16),
            pltpu.VMEM((2, 4, NX, PACK, W), BF16),
            pltpu.VMEM((2, 4, NX, PACK, W), BF16),
            pltpu.VMEM((3, PACK, W), BF16),
            pltpu.VMEM((NX, PACK, W), BF16),
            pltpu.VMEM((NX * W, K), BF16),
            pltpu.VMEM((4, NX * W, K), BF16),
            sem((5,)), sem((4, 2)), sem((4, 2)), sem((5, 3)), sem((5, 3)), sem((5, 4)), sem((5, 4)),
            sem((8,)), sem((8,)), sem((8,)), sem((8,)),
            sem((6,)), sem((6,)), sem((2, 4, NX)), sem((2, 4, NX)), sem((3,)), sem((3,)),
        ],
        compiler_params=pltpu.CompilerParams(
            collective_id=0, has_side_effects=True, vmem_limit_bytes=56 * 2**20),
        name="attend_project",
    )(queries, keys, values, doc_ids.reshape(1, T), w_out.T)


def solution(mesh):
    placed = (P("seq", "tp"), P("seq", "tp"), P("seq", "tp"), P("seq"), P("tp", "seq"))
    return jax.shard_map(
        local, mesh=mesh, in_specs=placed, out_specs=P("seq", "tp"), check_vma=False
    )
```

```python
import functools
import math

import jax
import jax.numpy as jnp
from jax import lax
from jax.experimental import pallas as pl
from jax.experimental.pallas import tpu as pltpu
from jax.sharding import PartitionSpec as P

MESH = pl.DeviceIdType.MESH
F32, BF16 = jnp.float32, jnp.bfloat16
NT = (((1,), (1,)), ((), ()))

NZ, NX, NY = 8, 4, 8
T = 192
HEADS = 5
W = 128
STAT = 16
KVR = T + STAT
DEPTH = 5
COLS = 80
K = HEADS * W
HALF = T // 2
GROUP = 48
PACK = T + GROUP
SCALE = math.log2(math.e) / math.sqrt(W)
HIDE = -131072.0


def dot_nt(a, b):
    return lax.dot_general(a, b, NT, preferred_element_type=F32)


def kernel(q_hbm, k_hbm, v_hbm, d_hbm, w_hbm, o_ref,
           kv, ff, qv, dv, qa, acc, top, wz, wr, ag, sbuf, rbuf, fsend, fin, selm, selr,
           in_s, kvz_s, kvz_r, kvx_s, kvx_r, kvm_s, kvm_r, kvd_s, kvd_r, wz_s, wz_r, wd_s, wd_r,
           ax_s, ax_r, rs_s, rs_r, fx_s, fx_r):
    s = lax.axis_index("seq")
    t = lax.axis_index("tp")
    z, x, c = s // 8, lax.rem(s // 2, 4), lax.rem(s, 2)
    me = x * 2 + c

    def dev(dz=0, dx=0, dc=0, dy=0):
        zz = lax.rem(z + dz + NZ, NZ)
        xx = lax.rem(x + dx + NX, NX)
        cc = lax.rem(c + dc, 2)
        return (zz * 8 + xx * 2 + cc, lax.rem(t + dy + NY, NY))

    up, right, left, across = dev(dz=1), dev(dx=1), dev(dx=-1), dev(dx=2)
    sib = dev(dc=1)
    xr, xl, xo = lax.rem(x + 1, NX), lax.rem(x + 3, NX), lax.rem(x + 2, NX)
    oc = 1 - c

    def rc(ref, ss, rs, to):
        return pltpu.make_async_remote_copy(
            src_ref=ref, dst_ref=ref, send_sem=ss, recv_sem=rs, device_id=to, device_id_type=MESH)

    barrier = pltpu.get_barrier_semaphore()
    peers = [dev(dz=i) for i in (1, -1, 2, -2)] + [right, left, across, sib] + [dev(dy=i) for i in (1, -1, 2, -2)]
    for peer in peers:
        pl.semaphore_signal(barrier, inc=1, device_id=peer, device_id_type=MESH)
    loads = [
        pltpu.make_async_copy(d_hbm, dv, in_s.at[0]),
        pltpu.make_async_copy(k_hbm, kv.at[0, c, x, pl.ds(0, T), pl.ds(0, W)], in_s.at[1]),
        pltpu.make_async_copy(v_hbm, kv.at[0, c, x, pl.ds(0, T), pl.ds(W, W)], in_s.at[2]),
        pltpu.make_async_copy(w_hbm, wz.at[z, c], in_s.at[3]),
        pltpu.make_async_copy(q_hbm, qv, in_s.at[4]),
    ]
    for load in loads:
        load.start()

    loads[0].wait()
    docs = jnp.broadcast_to(dv[...], (W, T))
    number = lax.broadcasted_iota(jnp.int32, (W, T), 0)
    first = jnp.sum((docs < number).astype(F32), axis=1, keepdims=True)
    last = jnp.sum((docs <= number).astype(F32), axis=1, keepdims=True)
    first = jnp.transpose(jnp.broadcast_to(first, (W, W)))
    last = jnp.transpose(jnp.broadcast_to(last, (W, W)))
    stat = jnp.concatenate([first[0:8], last[0:8]], axis=0).astype(BF16)
    kv[0, c, x, T:KVR, 0:W] = stat
    kv[0, c, x, T:KVR, W:2 * W] = jnp.zeros((STAT, W), BF16)
    loads[1].wait()
    loads[2].wait()

    pl.semaphore_wait(barrier, len(peers))

    started = []

    def go(copy):
        copy.start()
        started.append((copy, None))

    def go_if(cond, copy):
        @pl.when(cond)
        def _():
            copy.start()
        started.append((copy, cond))

    def z_copy(p, half):
        rows = pl.ds(0, 96) if half == 0 else pl.ds(96, KVR - 96)
        return pltpu.make_async_remote_copy(
            src_ref=kv.at[p, c, x, rows], dst_ref=kv.at[p + 1, c, x, rows], send_sem=kvz_s.at[p, half],
            recv_sem=kvz_r.at[p, half], device_id=up, device_id_type=MESH)

    def x_start(p):
        blk = kv.at[p, c, x]
        go(rc(blk, kvx_s.at[p, 0], kvx_r.at[p, 0], right))
        go(rc(blk, kvx_s.at[p, 1], kvx_r.at[p, 1], left))
        go(rc(blk, kvd_s.at[p, 0], kvd_r.at[p, 0], sib))

    low, high = pl.ds(0, 96), pl.ds(96, KVR - 96)

    def x_relay(p):
        ref = kv.at[p, c, xl]
        rc(ref, kvx_s.at[p, 0], kvx_r.at[p, 0], right).wait_recv()
        go(rc(kv.at[p, c, xl, low], kvx_s.at[p, 2], kvx_r.at[p, 2], right))
        go(rc(ref, kvd_s.at[p, 1], kvd_r.at[p, 1], sib))
        ref = kv.at[p, c, xr]
        rc(ref, kvx_s.at[p, 1], kvx_r.at[p, 1], left).wait_recv()
        go(rc(kv.at[p, c, xr, high], kvx_s.at[p, 3], kvx_r.at[p, 3], left))
        go(rc(ref, kvd_s.at[p, 2], kvd_r.at[p, 2], sib))

    def x_end(p):
        rc(kv.at[p, c, xo, low], kvx_s.at[p, 2], kvx_r.at[p, 2], right).wait_recv()
        rc(kv.at[p, c, xo, high], kvx_s.at[p, 3], kvx_r.at[p, 3], left).wait_recv()
        go(rc(kv.at[p, c, xo], kvd_s.at[p, 3], kvd_r.at[p, 3], sib))

    def x_start_mixed(p, half):
        rows = (low, high)[half]
        for i, (to, dest) in enumerate(((right, xr), (left, xl), (across, xo))):
            go_if((x < dest) if p == 0 else (x > dest),
                  rc(kv.at[p, c, x, rows], kvm_s.at[p // 4, half, i], kvm_r.at[half, i], to))
        if half == 1:
            go_if(c == (0 if p == 0 else 1), rc(kv.at[p, c, x], kvd_s.at[p, 0], kvd_r.at[0, 0], sib))

    def plane_of(p, xx):
        return p if p > 0 else jnp.where(xx < x, 0, 4)

    def x_end_mixed():
        for i, xx in enumerate((xl, xr, xo)):
            ref = kv.at[plane_of(0, xx), c, xx]
            for half, rows in enumerate((low, high)):
                rc(ref.at[rows], kvm_s.at[0, half, i], kvm_r.at[half, i], right).wait_recv()
            go(rc(ref, kvd_s.at[0, i + 1], kvd_r.at[0, i + 1], sib))

    def sib_wait(p):
        own = p if p > 0 else jnp.where(c == 1, 0, 4)
        for i, (pp, xx) in enumerate(((own, x), (plane_of(p, xl), xl), (plane_of(p, xr), xr), (plane_of(p, xo), xo))):
            rc(kv.at[pp, oc, xx], kvd_s.at[p, i], kvd_r.at[p, i], sib).wait_recv()

    def z_step(p):
        for half in range(2):
            z_copy(p - 1, half).wait_recv()
            if p < DEPTH - 1:
                go(z_copy(p, half))
            else:
                x_start_mixed(p, half)
        if p < DEPTH - 1:
            x_start(p)

    def w_send(offset, i, dz):
        go(rc(wz.at[lax.rem(z + offset, NZ), c], wz_s.at[i], wz_r.at[i], dev(dz=dz)))

    def w_recv(i):
        ref = wz.at[lax.rem(z + i, NZ), c]
        rc(ref, wz_s.at[i], wz_r.at[i], up).wait_recv()
        go(rc(ref, wd_s.at[i], wd_r.at[i], sib))

    go(z_copy(0, 0))
    go(z_copy(0, 1))
    x_start_mixed(0, 0)
    x_start_mixed(0, 1)
    loads[3].wait()
    w_send(0, 1, -1)
    w_send(0, 2, -2)
    go(rc(wz.at[z, c], wd_s.at[0], wd_r.at[0], sib))

    row = lax.broadcasted_iota(jnp.int32, (T, W), 0).astype(F32)

    def doc_rows(bounds):
        bounds = bounds.astype(F32)
        return jnp.where((row >= bounds[0:1]) & (row < bounds[8:9]), 1.0, 0.0)

    own_docs = doc_rows(stat)
    feature = jnp.where(own_docs > 0.5, 0.0, HIDE).astype(BF16)
    loads[4].wait()
    for u in range(2):
        for h in range(HEADS):
            rows = slice((u * HEADS + h) * HALF, (u * HEADS + h + 1) * HALF)
            qa[rows, 0:W] = qv[u * HALF:(u + 1) * HALF, h * W:(h + 1) * W]
            qa[rows, W:2 * W] = feature[u * HALF:(u + 1) * HALF]
    k_own = jnp.concatenate([kv[0, c, x, 0:T, 0:W], own_docs.astype(BF16)], axis=1)
    v_own = jnp.concatenate([kv[0, c, x, 0:T, W:2 * W], jnp.ones((T, W), BF16)], axis=1)
    wr[...] = jnp.zeros_like(wr)

    def diagonal(u):
        rows = slice(u * HEADS * HALF, (u + 1) * HEADS * HALF)
        at = lax.broadcasted_iota(jnp.int32, (HALF, T), 0) + u * HALF
        causal = at >= lax.broadcasted_iota(jnp.int32, (HALF, T), 1)
        scores = jnp.where(jnp.concatenate([causal] * HEADS, axis=0), dot_nt(qa[rows, :], k_own), -1e30)
        high = jnp.broadcast_to(jnp.max(scores, axis=1, keepdims=True) * SCALE, (HEADS * HALF, W))
        weights = jnp.exp2(scores * SCALE - high[:, 0:1]).astype(BF16)
        top[rows, :] = high
        acc[rows, :] = jnp.dot(weights, v_own, preferred_element_type=F32)

    def attend(blocks, valid, tile, after=None):
        count = len(blocks)
        for i, where in enumerate(blocks):
            docs_b = doc_rows(kv[where[0], where[1], where[2], T:KVR, 0:W])
            ff[i] = jnp.where(valid[i], docs_b, 1.0).astype(BF16)

        def score(u):
            keys = jnp.concatenate([kv[i[0], i[1], i[2], 0:T, 0:W] for i in blocks], axis=0)
            keys = jnp.concatenate([keys, ff[0:count].reshape(count * T, W)], axis=1)
            return dot_nt(qa[u * tile:(u + 1) * tile, :], keys)

        tiles = HEADS * T // tile
        ahead = score(0)
        for u in range(tiles):
            rows = slice(u * tile, (u + 1) * tile)
            scores = ahead
            if u + 1 < tiles:
                ahead = score(u + 1)
            old = top[rows, :]
            new = jnp.maximum(old, jnp.max(scores, axis=1, keepdims=True) * SCALE)
            weights = jnp.exp2(scores * SCALE - new[:, 0:1]).astype(BF16)
            vals = jnp.concatenate([kv[i[0], i[1], i[2], 0:T, W:2 * W] for i in blocks], axis=0)
            vals = jnp.concatenate([vals, jnp.ones((count * T, W), BF16)], axis=1)
            keep = jnp.exp2(old - new)
            acc[rows, :] = acc[rows, :] * jnp.concatenate([keep, keep], axis=1) + jnp.dot(
                weights, vals, preferred_element_type=F32)
            top[rows, :] = new
            if after is not None:
                after(u)

    def attend_plane(p):
        sib_wait(p)
        attend([(p, b // 4, b % 4) for b in range(8)], [z >= p] * 8, 320)

    def attend_mixed(core, after=None):
        early = [i * 2 + core < me for i in range(NX)]
        attend([(jnp.where(e, 0, 4), core, i) for i, e in enumerate(early)], [e | (z >= 4) for e in early], 480, after)

    def a_send(u):
        mine = slice(u * HALF, (u + 1) * HALF)
        for h in range(HEADS):
            rows = slice((u * HEADS + h) * HALF, (u * HEADS + h + 1) * HALF)
            ag[0, mine, h * W:(h + 1) * W] = (acc[rows, 0:W] / acc[rows, W:2 * W]).astype(BF16)
        for i, to in enumerate((right, left)):
            go(pltpu.make_async_remote_copy(
                src_ref=ag.at[0, pl.ds(u * HALF, HALF)], dst_ref=ag.at[1 + u, pl.ds(i * HALF, HALF)],
                send_sem=ax_s.at[u, i], recv_sem=ax_r.at[u, i], device_id=to, device_id_type=MESH))

    def a_far_copy(u, i):
        return pltpu.make_async_remote_copy(
            src_ref=ag.at[1 + u, pl.ds(i * (HALF + GROUP), GROUP)],
            dst_ref=ag.at[3, pl.ds(u * HALF + i * GROUP, GROUP)],
            send_sem=ax_s.at[u, 2 + i], recv_sem=ax_r.at[u, 2 + i],
            device_id=(right, left)[i], device_id_type=MESH)

    def a_near(u):
        for i in range(2):
            rc(ag.at[1 + u, pl.ds(i * HALF, HALF)], ax_s.at[u, i], ax_r.at[u, i], right).wait_recv()
            go(a_far_copy(u, i))

    def a_far():
        for u in range(2):
            for i in range(2):
                a_far_copy(u, i).wait_recv()

    def w_ready(i):
        plane = lax.rem(z + i, NZ)
        rc(wz.at[plane, oc], wd_s.at[i], wd_r.at[i], sib).wait_recv()
        for g in range(4):
            wr[plane, 32 * g:32 * g + 16, g * K:(g + 1) * K] = wz[plane, 0, 64:80, :]
            wr[plane, 32 * g + 16:32 * g + 32, g * K:(g + 1) * K] = wz[plane, 1, 64:80, :]

    z_step(1)
    diagonal(0)
    z_step(2)
    x_relay(1)
    z_step(3)
    w_send(0, 7, 1)
    w_send(0, 6, 2)
    diagonal(1)
    x_end(1)
    x_relay(2)
    w_recv(2)
    w_send(2, 3, -1)
    w_send(2, 4, -2)
    attend_plane(1)
    z_step(4)
    x_end(2)
    x_relay(3)
    attend_plane(2)
    x_end(3)
    w_recv(6)
    w_send(6, 5, 1)
    attend_plane(3)
    x_end_mixed()
    for i in (1, 7, 3, 4):
        w_recv(i)
    attend_mixed(c)
    w_recv(5)
    for i in (0, 1, 2, 3, 4, 6, 7):
        w_ready(i)
    sib_wait(0)
    attend_mixed(oc, a_send)
    w_ready(5)

    def partial(j, o):
        cols = jnp.concatenate([wz[o, 0, 0:64, :], wz[o, 1, 0:64, :]], axis=0)
        main = dot_nt(ag[j], cols)
        rows = jnp.concatenate([ag[j, g * GROUP:(g + 1) * GROUP, :] for g in range(4)], axis=1)
        rest = dot_nt(rows, wr[o])
        return jnp.concatenate([main[0:HALF], rest, main[HALF:T]], axis=0)

    y_up, y_down = dev(dy=1), dev(dy=-1)

    def hops(d, j):
        return 4 if (d + j) % 2 == 1 else 3

    def rs(d, r, j):
        leap = 2 if (j == 3 and r == 4) else 1
        return pltpu.make_async_remote_copy(
            src_ref=sbuf.at[d, r - 1, j], dst_ref=rbuf.at[d, r - 1, j],
            send_sem=rs_s.at[d, r - 1, j], recv_sem=rs_r.at[d, r - 1, j],
            device_id=dev(dy=leap if d == 0 else -leap), device_id_type=MESH)

    def send_block(d, r, j, arrived):
        total = partial(j, lax.rem(t + r, NY) if d == 0 else lax.rem(t - r + NY, NY))
        for i in arrived:
            rs(d, i, j).wait_recv()
            total = total + rbuf[d, i - 1, j].astype(F32)
        sbuf[d, r - 1, j] = total.astype(BF16)
        go(rs(d, r, j))

    def send_step(n, j):
        for d in range(2):
            if j == 3 and hops(d, j) == 4:
                if n == 0:
                    send_block(d, 4, j, ())
                r = 3 - n
                arrived = () if n == 0 else (4, 3) if n == 1 else (2,)
            else:
                r = hops(d, j) - n
                arrived = () if n == 0 else (r + 1,)
            if r > 0:
                send_block(d, r, j, arrived)

    def fx(j, i):
        to, slot, half = ((), ((left, 1, 0), (right, 3, 0)), ((left, 1, 1), (right, 3, 1)), ((across, 2, 0), (across, 2, 1)))[j][i]
        return pltpu.make_async_remote_copy(
            src_ref=fsend.at[j - 1, pl.ds(i * HALF, HALF + GROUP)], dst_ref=fin.at[slot, half],
            send_sem=fx_s.at[2 * slot + half - 2], recv_sem=fx_r.at[2 * slot + half - 2],
            device_id=to, device_id_type=MESH)

    def finish(j):
        total = partial(j, t)
        for d in range(2):
            rs(d, 1, j).wait_recv()
            total = total + rbuf[d, 0, j].astype(F32)
        total = total.astype(BF16)
        if j == 0:
            fin[0, 0] = total[0:HALF + GROUP]
            fin[0, 1] = total[HALF:PACK]
        else:
            fsend[j - 1] = total
            go(fx(j, 0))
            go(fx(j, 1))

    def second(slot, half):
        return slot == 3 or (slot != 1 and half == 1)

    send_step(0, 0)
    a_near(0)
    send_step(0, 1)

    lane = lax.broadcasted_iota(jnp.int32, (W, K), 0)
    spot = lax.rem(lane, 32)
    main_at = lane + jnp.where(lane < 64, 0, 16)
    rest_at = spot + jnp.where(spot < 16, 64, 128)
    for i in range(NX):
        col = lax.broadcasted_iota(jnp.int32, (W, K), 1) - lax.rem(x + i, NX) * 160
        rows = slice(i * W, (i + 1) * W)
        selm[rows, :] = jnp.where(col == main_at, 1.0, 0.0).astype(BF16)
        for u in range(2):
            for g in range(2):
                here = lane // 32 == g + (2 if second(i, u) else 0)
                selr[2 * u + g, rows, :] = jnp.where((col == rest_at) & here, 1.0, 0.0).astype(BF16)

    send_step(1, 0)
    a_near(1)
    send_step(0, 2)
    send_step(1, 1)
    send_step(2, 0)
    a_far()
    send_step(0, 3)
    send_step(1, 2)
    send_step(2, 1)
    send_step(1, 3)
    send_step(2, 2)
    send_step(3, 1)
    send_step(2, 3)
    send_step(3, 2)
    send_step(3, 0)
    finish(1)
    finish(2)
    finish(3)
    finish(0)
    for j in (1, 2, 3):
        for i in range(2):
            fx(j, i).wait_recv()

    def main_of(i, u):
        return fin[i, u, GROUP:GROUP + HALF, :] if second(i, u) else fin[i, u, 0:HALF, :]

    def rest_of(i, u):
        return fin[i, u, 0:GROUP, :] if second(i, u) else fin[i, u, HALF:HALF + GROUP, :]

    for u in range(2):
        main = jnp.dot(jnp.concatenate([main_of(i, u) for i in range(NX)], axis=1), selm[...], preferred_element_type=F32)
        rest = jnp.concatenate([rest_of(i, u) for i in range(NX)], axis=1)
        for g in range(2):
            add = jnp.dot(rest, selr[2 * u + g], preferred_element_type=F32)
            o_ref[u * HALF + g * GROUP:u * HALF + (g + 1) * GROUP, :] = (
                main[g * GROUP:(g + 1) * GROUP] + add).astype(BF16)

    for copy, cond in started:
        if cond is None:
            copy.wait_send()
        else:
            pl.when(cond)(copy.wait_send)


def local(queries, keys, values, doc_ids, w_out):
    sem = pltpu.SemaphoreType.DMA
    vmem = pl.BlockSpec(memory_space=pltpu.VMEM)
    return pl.pallas_call(
        kernel,
        out_shape=pltpu.VMEM((T, K), BF16),
        in_specs=[pl.BlockSpec(memory_space=pl.ANY)] * 5,
        out_specs=vmem,
        scratch_shapes=[
            pltpu.VMEM((DEPTH, 2, NX, KVR, 2 * W), BF16),
            pltpu.VMEM((8, T, W), BF16),
            pltpu.VMEM((T, K), BF16),
            pltpu.VMEM((1, T), jnp.int32),
            pltpu.VMEM((HEADS * T, 2 * W), BF16),
            pltpu.VMEM((HEADS * T, 2 * W), F32),
            pltpu.VMEM((HEADS * T, W), F32),
            pltpu.VMEM((NZ, 2, COLS, K), BF16),
            pltpu.VMEM((NY, W, 4 * K), BF16),
            pltpu.VMEM((NX, T, K), BF16),
            pltpu.VMEM((2, 4, NX, PACK, W), BF16),
            pltpu.VMEM((2, 4, NX, PACK, W), BF16),
            pltpu.VMEM((3, PACK, W), BF16),
            pltpu.VMEM((NX, 2, HALF + GROUP, W), BF16),
            pltpu.VMEM((NX * W, K), BF16),
            pltpu.VMEM((4, NX * W, K), BF16),
            sem((5,)), sem((4, 2)), sem((4, 2)), sem((4, 4)), sem((4, 4)), sem((2, 2, 3)), sem((2, 3)), sem((5, 4)), sem((5, 4)),
            sem((8,)), sem((8,)), sem((8,)), sem((8,)),
            sem((2, 4)), sem((2, 4)), sem((2, 4, NX)), sem((2, 4, NX)), sem((6,)), sem((6,)),
        ],
        compiler_params=pltpu.CompilerParams(
            collective_id=0, has_side_effects=True, vmem_limit_bytes=56 * 2**20),
        name="attend_project",
    )(queries, keys, values, doc_ids.reshape(1, T), w_out.T)


def solution(mesh):
    placed = (P("seq", "tp"), P("seq", "tp"), P("seq", "tp"), P("seq"), P("tp", "seq"))
    return jax.shard_map(
        local, mesh=mesh, in_specs=placed, out_specs=P("seq", "tp"), check_vma=False
    )
```

```python
import functools
import math

import jax
import jax.numpy as jnp
from jax import lax
from jax.experimental import pallas as pl
from jax.experimental.pallas import tpu as pltpu
from jax.sharding import PartitionSpec as P

MESH = pl.DeviceIdType.MESH
F32, BF16 = jnp.float32, jnp.bfloat16
NT = (((1,), (1,)), ((), ()))

NZ, NX, NY = 8, 4, 8
T = 192
HEADS = 5
W = 128
STAT = 16
KVR = T + STAT
DEPTH = 5
COLS = 80
K = HEADS * W
HALF = T // 2
GROUP = 48
PACK = T + GROUP
SCALE = math.log2(math.e) / math.sqrt(W)
HIDE = -131072.0


def dot_nt(a, b):
    return lax.dot_general(a, b, NT, preferred_element_type=F32)


def kernel(q_hbm, k_hbm, v_hbm, d_hbm, w_hbm, o_ref,
           kv, ff, qv, dv, qa, acc, top, wz, wr, ag, sbuf, rbuf, fsend, fin, selm, selr, out,
           in_s, kvz_s, kvz_r, kvx_s, kvx_r, kvm_s, kvm_r, kvd_s, kvd_r, wz_s, wz_r, wd_s, wd_r,
           ax_s, ax_r, rs_s, rs_r, fx_s, fx_r):
    s = lax.axis_index("seq")
    t = lax.axis_index("tp")
    z, x, c = s // 8, lax.rem(s // 2, 4), lax.rem(s, 2)
    me = x * 2 + c

    def dev(dz=0, dx=0, dc=0, dy=0):
        zz = lax.rem(z + dz + NZ, NZ)
        xx = lax.rem(x + dx + NX, NX)
        cc = lax.rem(c + dc, 2)
        return (zz * 8 + xx * 2 + cc, lax.rem(t + dy + NY, NY))

    up, right, left, across = dev(dz=1), dev(dx=1), dev(dx=-1), dev(dx=2)
    sib = dev(dc=1)
    xr, xl, xo = lax.rem(x + 1, NX), lax.rem(x + 3, NX), lax.rem(x + 2, NX)
    oc = 1 - c

    def rc(ref, ss, rs, to):
        return pltpu.make_async_remote_copy(
            src_ref=ref, dst_ref=ref, send_sem=ss, recv_sem=rs, device_id=to, device_id_type=MESH)

    barrier = pltpu.get_barrier_semaphore()
    peers = [dev(dz=i) for i in (1, -1, 2, -2)] + [right, left, across, sib] + [dev(dy=i) for i in (1, -1, 2, -2)]
    for peer in peers:
        pl.semaphore_signal(barrier, inc=1, device_id=peer, device_id_type=MESH)
    loads = [
        pltpu.make_async_copy(d_hbm, dv, in_s.at[0]),
        pltpu.make_async_copy(k_hbm, kv.at[0, c, x, pl.ds(0, T), pl.ds(0, W)], in_s.at[1]),
        pltpu.make_async_copy(v_hbm, kv.at[0, c, x, pl.ds(0, T), pl.ds(W, W)], in_s.at[2]),
        pltpu.make_async_copy(w_hbm, wz.at[z, c], in_s.at[3]),
        pltpu.make_async_copy(q_hbm, qv, in_s.at[4]),
    ]
    for load in loads:
        load.start()

    loads[1].wait()
    loads[2].wait()

    pl.semaphore_wait(barrier, len(peers))

    started = []

    def go(copy):
        copy.start()
        started.append((copy, None))

    def go_if(cond, copy):
        @pl.when(cond)
        def _():
            copy.start()
        started.append((copy, cond))

    def z_copy(p, half):
        rows = pl.ds(0, 96) if half == 0 else pl.ds(96, KVR - 96)
        return pltpu.make_async_remote_copy(
            src_ref=kv.at[p, c, x, rows], dst_ref=kv.at[p + 1, c, x, rows], send_sem=kvz_s.at[p, half],
            recv_sem=kvz_r.at[p, half], device_id=up, device_id_type=MESH)

    def x_start(p):
        blk = kv.at[p, c, x]
        go(rc(blk, kvx_s.at[p, 0], kvx_r.at[p, 0], right))
        go(rc(blk, kvx_s.at[p, 1], kvx_r.at[p, 1], left))
        go(rc(blk, kvd_s.at[p, 0], kvd_r.at[p, 0], sib))

    low, high = pl.ds(0, 96), pl.ds(96, KVR - 96)

    def x_relay(p):
        ref = kv.at[p, c, xl]
        rc(ref, kvx_s.at[p, 0], kvx_r.at[p, 0], right).wait_recv()
        go(rc(kv.at[p, c, xl, low], kvx_s.at[p, 2], kvx_r.at[p, 2], right))
        go(rc(ref, kvd_s.at[p, 1], kvd_r.at[p, 1], sib))
        ref = kv.at[p, c, xr]
        rc(ref, kvx_s.at[p, 1], kvx_r.at[p, 1], left).wait_recv()
        go(rc(kv.at[p, c, xr, high], kvx_s.at[p, 3], kvx_r.at[p, 3], left))
        go(rc(ref, kvd_s.at[p, 2], kvd_r.at[p, 2], sib))

    def x_end(p):
        rc(kv.at[p, c, xo, low], kvx_s.at[p, 2], kvx_r.at[p, 2], right).wait_recv()
        rc(kv.at[p, c, xo, high], kvx_s.at[p, 3], kvx_r.at[p, 3], left).wait_recv()
        go(rc(kv.at[p, c, xo], kvd_s.at[p, 3], kvd_r.at[p, 3], sib))

    def x_start_mixed(p, half):
        rows = (low, high)[half]
        for i, (to, dest) in enumerate(((right, xr), (left, xl), (across, xo))):
            go_if((x < dest) if p == 0 else (x > dest),
                  rc(kv.at[p, c, x, rows], kvm_s.at[p // 4, half, i], kvm_r.at[half, i], to))
        if half == 1:
            go_if(c == (0 if p == 0 else 1), rc(kv.at[p, c, x], kvd_s.at[p, 0], kvd_r.at[0, 0], sib))

    def plane_of(p, xx):
        return p if p > 0 else jnp.where(xx < x, 0, 4)

    def x_end_mixed():
        for i, xx in enumerate((xl, xr, xo)):
            ref = kv.at[plane_of(0, xx), c, xx]
            for half, rows in enumerate((low, high)):
                rc(ref.at[rows], kvm_s.at[0, half, i], kvm_r.at[half, i], right).wait_recv()
            go(rc(ref, kvd_s.at[0, i + 1], kvd_r.at[0, i + 1], sib))

    def sib_wait(p):
        own = p if p > 0 else jnp.where(c == 1, 0, 4)
        for i, (pp, xx) in enumerate(((own, x), (plane_of(p, xl), xl), (plane_of(p, xr), xr), (plane_of(p, xo), xo))):
            rc(kv.at[pp, oc, xx], kvd_s.at[p, i], kvd_r.at[p, i], sib).wait_recv()

    def z_step(p):
        for half in range(2):
            z_copy(p - 1, half).wait_recv()
            if p < DEPTH - 1:
                go(z_copy(p, half))
            else:
                x_start_mixed(p, half)
        if p < DEPTH - 1:
            x_start(p)

    def w_send(offset, i, dz):
        go(rc(wz.at[lax.rem(z + offset, NZ), c], wz_s.at[i], wz_r.at[i], dev(dz=dz)))

    def w_recv(i):
        ref = wz.at[lax.rem(z + i, NZ), c]
        rc(ref, wz_s.at[i], wz_r.at[i], up).wait_recv()
        go(rc(ref, wd_s.at[i], wd_r.at[i], sib))

    go(z_copy(0, 0))
    x_start_mixed(0, 0)

    loads[0].wait()
    docs = jnp.broadcast_to(dv[...], (W, T))
    number = lax.broadcasted_iota(jnp.int32, (W, T), 0)
    first = jnp.sum((docs < number).astype(F32), axis=1, keepdims=True)
    last = jnp.sum((docs <= number).astype(F32), axis=1, keepdims=True)
    first = jnp.transpose(jnp.broadcast_to(first, (W, W)))
    last = jnp.transpose(jnp.broadcast_to(last, (W, W)))
    stat = jnp.concatenate([first[0:8], last[0:8]], axis=0).astype(BF16)
    kv[0, c, x, T:KVR, 0:W] = stat
    kv[0, c, x, T:KVR, W:2 * W] = jnp.zeros((STAT, W), BF16)

    go(z_copy(0, 1))
    x_start_mixed(0, 1)
    loads[3].wait()
    w_send(0, 1, -1)
    w_send(0, 2, -2)
    go(rc(wz.at[z, c], wd_s.at[0], wd_r.at[0], sib))

    row = lax.broadcasted_iota(jnp.int32, (T, W), 0).astype(F32)

    def doc_rows(bounds):
        bounds = bounds.astype(F32)
        return jnp.where((row >= bounds[0:1]) & (row < bounds[8:9]), 1.0, 0.0)

    own_docs = doc_rows(stat)
    feature = jnp.where(own_docs > 0.5, 0.0, HIDE).astype(BF16)
    loads[4].wait()
    for u in range(2):
        for h in range(HEADS):
            rows = slice((u * HEADS + h) * HALF, (u * HEADS + h + 1) * HALF)
            qa[rows, 0:W] = qv[u * HALF:(u + 1) * HALF, h * W:(h + 1) * W]
            qa[rows, W:2 * W] = feature[u * HALF:(u + 1) * HALF]
    k_own = jnp.concatenate([kv[0, c, x, 0:T, 0:W], own_docs.astype(BF16)], axis=1)
    v_own = jnp.concatenate([kv[0, c, x, 0:T, W:2 * W], jnp.ones((T, W), BF16)], axis=1)
    wr[...] = jnp.zeros_like(wr)

    def diagonal(u):
        rows = slice(u * HEADS * HALF, (u + 1) * HEADS * HALF)
        at = lax.broadcasted_iota(jnp.int32, (HALF, T), 0) + u * HALF
        causal = at >= lax.broadcasted_iota(jnp.int32, (HALF, T), 1)
        scores = jnp.where(jnp.concatenate([causal] * HEADS, axis=0), dot_nt(qa[rows, :], k_own), -1e30)
        high = jnp.broadcast_to(jnp.max(scores, axis=1, keepdims=True) * SCALE, (HEADS * HALF, W))
        weights = jnp.exp2(scores * SCALE - high[:, 0:1]).astype(BF16)
        top[rows, :] = high
        acc[rows, :] = jnp.dot(weights, v_own, preferred_element_type=F32)

    def attend(blocks, valid, tile, after=None):
        count = len(blocks)
        for i, where in enumerate(blocks):
            docs_b = doc_rows(kv[where[0], where[1], where[2], T:KVR, 0:W])
            ff[i] = jnp.where(valid[i], docs_b, 1.0).astype(BF16)

        def score(u):
            keys = jnp.concatenate([kv[i[0], i[1], i[2], 0:T, 0:W] for i in blocks], axis=0)
            keys = jnp.concatenate([keys, ff[0:count].reshape(count * T, W)], axis=1)
            return dot_nt(qa[u * tile:(u + 1) * tile, :], keys)

        tiles = HEADS * T // tile
        ahead = score(0)
        for u in range(tiles):
            rows = slice(u * tile, (u + 1) * tile)
            scores = ahead
            if u + 1 < tiles:
                ahead = score(u + 1)
            old = top[rows, :]
            new = jnp.maximum(old, jnp.max(scores, axis=1, keepdims=True) * SCALE)
            weights = jnp.exp2(scores * SCALE - new[:, 0:1]).astype(BF16)
            vals = jnp.concatenate([kv[i[0], i[1], i[2], 0:T, W:2 * W] for i in blocks], axis=0)
            vals = jnp.concatenate([vals, jnp.ones((count * T, W), BF16)], axis=1)
            keep = jnp.exp2(old - new)
            acc[rows, :] = acc[rows, :] * jnp.concatenate([keep, keep], axis=1) + jnp.dot(
                weights, vals, preferred_element_type=F32)
            top[rows, :] = new
            if after is not None:
                after(u)

    def attend_plane(p):
        sib_wait(p)
        attend([(p, b // 4, b % 4) for b in range(8)], [z >= p] * 8, 320)

    def attend_mixed(core, after=None):
        early = [i * 2 + core < me for i in range(NX)]
        attend([(jnp.where(e, 0, 4), core, i) for i, e in enumerate(early)], [e | (z >= 4) for e in early], 480, after)

    def a_copy(u, i):
        return pltpu.make_async_remote_copy(
            src_ref=ag.at[0, pl.ds(u * HALF, HALF)], dst_ref=ag.at[1 + u, pl.ds(i * HALF, HALF)],
            send_sem=ax_s.at[u, i], recv_sem=ax_r.at[u, i], device_id=(right, left)[i], device_id_type=MESH)

    def a_send(u):
        mine = slice(u * HALF, (u + 1) * HALF)
        for h in range(HEADS):
            rows = slice((u * HEADS + h) * HALF, (u * HEADS + h + 1) * HALF)
            ag[0, mine, h * W:(h + 1) * W] = (acc[rows, 0:W] / acc[rows, W:2 * W]).astype(BF16)
        if u == 0:
            a_copy(0, 0).start()
            a_copy(0, 1).start()

    def a_far_copy(u, i):
        return pltpu.make_async_remote_copy(
            src_ref=ag.at[1 + u, pl.ds(i * (HALF + GROUP), GROUP)],
            dst_ref=ag.at[3, pl.ds(u * HALF + i * GROUP, GROUP)],
            send_sem=ax_s.at[u, 2 + i], recv_sem=ax_r.at[u, 2 + i],
            device_id=(right, left)[i], device_id_type=MESH)

    def a_near(u):
        for i in range(2):
            rc(ag.at[1 + u, pl.ds(i * HALF, HALF)], ax_s.at[u, i], ax_r.at[u, i], right).wait_recv()
            go(a_far_copy(u, i))

    def a_far():
        for u in range(2):
            for i in range(2):
                a_far_copy(u, i).wait_recv()

    def w_ready(i):
        plane = lax.rem(z + i, NZ)
        rc(wz.at[plane, oc], wd_s.at[i], wd_r.at[i], sib).wait_recv()
        for g in range(4):
            wr[plane, 32 * g:32 * g + 16, g * K:(g + 1) * K] = wz[plane, 0, 64:80, :]
            wr[plane, 32 * g + 16:32 * g + 32, g * K:(g + 1) * K] = wz[plane, 1, 64:80, :]

    z_step(1)
    diagonal(0)
    z_step(2)
    x_relay(1)
    z_step(3)
    w_send(0, 7, 1)
    w_send(0, 6, 2)
    diagonal(1)
    x_end(1)
    x_relay(2)
    w_recv(2)
    w_send(2, 3, -1)
    w_send(2, 4, -2)
    z_step(4)
    attend_plane(1)
    x_end(2)
    x_relay(3)
    attend_plane(2)
    x_end(3)
    w_recv(6)
    w_send(6, 5, 1)
    attend_plane(3)
    x_end_mixed()
    for i in (1, 7, 3, 4):
        w_recv(i)
    attend_mixed(c)
    w_recv(5)
    for i in (0, 1, 2, 3, 4, 6, 7):
        w_ready(i)
    sib_wait(0)
    attend_mixed(oc, a_send)
    w_ready(5)

    def partial(j, o):
        cols = jnp.concatenate([wz[o, 0, 0:64, :], wz[o, 1, 0:64, :]], axis=0)
        main = dot_nt(ag[j], cols)
        rows = jnp.concatenate([ag[j, g * GROUP:(g + 1) * GROUP, :] for g in range(4)], axis=1)
        rest = dot_nt(rows, wr[o])
        return jnp.concatenate([main[0:HALF], rest, main[HALF:T]], axis=0)

    y_up, y_down = dev(dy=1), dev(dy=-1)

    def hops(d, j):
        return 4 if (d + j) % 2 == 1 else 3

    def rs(d, r, j):
        leap = 2 if (j == 3 and r == 4) else 1
        return pltpu.make_async_remote_copy(
            src_ref=sbuf.at[d, r - 1, j], dst_ref=rbuf.at[d, r - 1, j],
            send_sem=rs_s.at[d, r - 1, j], recv_sem=rs_r.at[d, r - 1, j],
            device_id=dev(dy=leap if d == 0 else -leap), device_id_type=MESH)

    def send_block(d, r, j, arrived):
        total = partial(j, lax.rem(t + r, NY) if d == 0 else lax.rem(t - r + NY, NY))
        for i in arrived:
            rs(d, i, j).wait_recv()
            total = total + rbuf[d, i - 1, j].astype(F32)
        sbuf[d, r - 1, j] = total.astype(BF16)
        go(rs(d, r, j))

    def send_step(n, j):
        for d in range(2):
            if j == 3 and hops(d, j) == 4:
                if n == 0:
                    send_block(d, 4, j, ())
                r = 3 - n
                arrived = () if n == 0 else (4, 3) if n == 1 else (2,)
            else:
                r = hops(d, j) - n
                arrived = () if n == 0 else (r + 1,)
            if r > 0:
                send_block(d, r, j, arrived)

    def fx(j, i):
        to, slot, half = ((), ((left, 1, 0), (right, 3, 0)), ((left, 1, 1), (right, 3, 1)), ((across, 2, 0), (across, 2, 1)))[j][i]
        return pltpu.make_async_remote_copy(
            src_ref=fsend.at[j - 1, pl.ds(i * HALF, HALF + GROUP)], dst_ref=fin.at[slot, half],
            send_sem=fx_s.at[2 * slot + half - 2], recv_sem=fx_r.at[2 * slot + half - 2],
            device_id=to, device_id_type=MESH)

    def finish(j):
        total = partial(j, t)
        for d in range(2):
            rs(d, 1, j).wait_recv()
            total = total + rbuf[d, 0, j].astype(F32)
        total = total.astype(BF16)
        if j == 0:
            fin[0, 0] = total[0:HALF + GROUP]
            fin[0, 1] = total[HALF:PACK]
        else:
            fsend[j - 1] = total
            go(fx(j, 0))
            go(fx(j, 1))

    def second(slot, half):
        return slot == 3 or (slot != 1 and half == 1)

    send_step(0, 0)
    for i in range(2):
        a_copy(0, i).wait_send()
        go(a_copy(1, i))
    a_near(0)
    send_step(0, 1)

    lane = lax.broadcasted_iota(jnp.int32, (W, K), 0)
    spot = lax.rem(lane, 32)
    main_at = lane + jnp.where(lane < 64, 0, 16)
    rest_at = spot + jnp.where(spot < 16, 64, 128)
    for i in range(NX):
        col = lax.broadcasted_iota(jnp.int32, (W, K), 1) - lax.rem(x + i, NX) * 160
        rows = slice(i * W, (i + 1) * W)
        selm[rows, :] = jnp.where(col == main_at, 1.0, 0.0).astype(BF16)
        for u in range(2):
            for g in range(2):
                here = lane // 32 == g + (2 if second(i, u) else 0)
                selr[2 * u + g, rows, :] = jnp.where((col == rest_at) & here, 1.0, 0.0).astype(BF16)

    send_step(1, 0)
    a_near(1)
    send_step(0, 2)
    send_step(1, 1)
    send_step(2, 0)
    a_far()
    send_step(0, 3)
    send_step(1, 2)
    send_step(2, 1)
    send_step(1, 3)
    send_step(2, 2)
    send_step(3, 1)
    send_step(2, 3)
    send_step(3, 2)
    send_step(3, 0)
    finish(1)
    finish(3)
    finish(2)
    finish(0)

    def main_of(i, u):
        return fin[i, u, GROUP:GROUP + HALF, :] if second(i, u) else fin[i, u, 0:HALF, :]

    def rest_of(i, u):
        return fin[i, u, 0:GROUP, :] if second(i, u) else fin[i, u, HALF:HALF + GROUP, :]

    def place(slots):
        lanes = slice(slots[0] * W, (slots[-1] + 1) * W)
        halves = []
        for u in range(2):
            main = jnp.dot(jnp.concatenate([main_of(i, u) for i in slots], axis=1), selm[lanes, :], preferred_element_type=F32)
            rest = jnp.concatenate([rest_of(i, u) for i in slots], axis=1)
            add = [jnp.dot(rest, selr[2 * u + g, lanes, :], preferred_element_type=F32) for g in range(2)]
            halves.append(main + jnp.concatenate(add, axis=0))
        return jnp.concatenate(halves, axis=0)

    for i in range(2):
        fx(3, i).wait_recv()
    out[...] = place((2,))
    fx(1, 0).wait_recv()
    fx(2, 0).wait_recv()
    out[...] += place((0, 1))
    fx(1, 1).wait_recv()
    fx(2, 1).wait_recv()
    o_ref[...] = (out[...] + place((3,))).astype(BF16)

    for copy, cond in started:
        if cond is None:
            copy.wait_send()
        else:
            pl.when(cond)(copy.wait_send)


def local(queries, keys, values, doc_ids, w_out):
    sem = pltpu.SemaphoreType.DMA
    vmem = pl.BlockSpec(memory_space=pltpu.VMEM)
    return pl.pallas_call(
        kernel,
        out_shape=pltpu.VMEM((T, K), BF16),
        in_specs=[pl.BlockSpec(memory_space=pl.ANY)] * 5,
        out_specs=vmem,
        scratch_shapes=[
            pltpu.VMEM((DEPTH, 2, NX, KVR, 2 * W), BF16),
            pltpu.VMEM((8, T, W), BF16),
            pltpu.VMEM((T, K), BF16),
            pltpu.VMEM((1, T), jnp.int32),
            pltpu.VMEM((HEADS * T, 2 * W), BF16),
            pltpu.VMEM((HEADS * T, 2 * W), F32),
            pltpu.VMEM((HEADS * T, W), F32),
            pltpu.VMEM((NZ, 2, COLS, K), BF16),
            pltpu.VMEM((NY, W, 4 * K), BF16),
            pltpu.VMEM((NX, T, K), BF16),
            pltpu.VMEM((2, 4, NX, PACK, W), BF16),
            pltpu.VMEM((2, 4, NX, PACK, W), BF16),
            pltpu.VMEM((3, PACK, W), BF16),
            pltpu.VMEM((NX, 2, HALF + GROUP, W), BF16),
            pltpu.VMEM((NX * W, K), BF16),
            pltpu.VMEM((4, NX * W, K), BF16),
            pltpu.VMEM((T, K), F32),
            sem((5,)), sem((4, 2)), sem((4, 2)), sem((4, 4)), sem((4, 4)), sem((2, 2, 3)), sem((2, 3)), sem((5, 4)), sem((5, 4)),
            sem((8,)), sem((8,)), sem((8,)), sem((8,)),
            sem((2, 4)), sem((2, 4)), sem((2, 4, NX)), sem((2, 4, NX)), sem((6,)), sem((6,)),
        ],
        compiler_params=pltpu.CompilerParams(
            collective_id=0, has_side_effects=True, vmem_limit_bytes=56 * 2**20),
        name="attend_project",
    )(queries, keys, values, doc_ids.reshape(1, T), w_out.T)


def solution(mesh):
    placed = (P("seq", "tp"), P("seq", "tp"), P("seq", "tp"), P("seq"), P("tp", "seq"))
    return jax.shard_map(
        local, mesh=mesh, in_specs=placed, out_specs=P("seq", "tp"), check_vma=False
    )
```

```python
import functools
import math

import jax
import jax.numpy as jnp
from jax import lax
from jax.experimental import pallas as pl
from jax.experimental.pallas import tpu as pltpu
from jax.sharding import PartitionSpec as P

MESH = pl.DeviceIdType.MESH
F32, BF16 = jnp.float32, jnp.bfloat16
NT = (((1,), (1,)), ((), ()))

NZ, NX, NY = 8, 4, 8
T = 192
HEADS = 5
W = 128
STAT = 16
KVR = T + STAT
DEPTH = 5
COLS = 80
K = HEADS * W
HALF = T // 2
GROUP = 48
PACK = T + GROUP
SCALE = math.log2(math.e) / math.sqrt(W)
HIDE = -131072.0


def dot_nt(a, b):
    return lax.dot_general(a, b, NT, preferred_element_type=F32)


def kernel(q_hbm, k_hbm, v_hbm, d_hbm, w_hbm, o_ref,
           kv, ff, qv, dv, qa, acc, top, wz, wr, ag, sbuf, rbuf, fsend, fin, selm, selr, out,
           in_s, kvz_s, kvz_r, kvx_s, kvx_r, kvm_s, kvm_r, kvd_s, kvd_r, wz_s, wz_r, wd_s, wd_r,
           ax_s, ax_r, rs_s, rs_r, fx_s, fx_r):
    s = lax.axis_index("seq")
    t = lax.axis_index("tp")
    z, x, c = s // 8, lax.rem(s // 2, 4), lax.rem(s, 2)
    me = x * 2 + c

    def dev(dz=0, dx=0, dc=0, dy=0):
        zz = lax.rem(z + dz + NZ, NZ)
        xx = lax.rem(x + dx + NX, NX)
        cc = lax.rem(c + dc, 2)
        return (zz * 8 + xx * 2 + cc, lax.rem(t + dy + NY, NY))

    up, right, left, across = dev(dz=1), dev(dx=1), dev(dx=-1), dev(dx=2)
    sib = dev(dc=1)
    xr, xl, xo = lax.rem(x + 1, NX), lax.rem(x + 3, NX), lax.rem(x + 2, NX)
    oc = 1 - c

    def rc(ref, ss, rs, to):
        return pltpu.make_async_remote_copy(
            src_ref=ref, dst_ref=ref, send_sem=ss, recv_sem=rs, device_id=to, device_id_type=MESH)

    barrier = pltpu.get_barrier_semaphore()
    peers = [dev(dz=i) for i in (1, -1, 2, -2)] + [right, left, across, sib] + [dev(dy=i) for i in (1, -1)]
    for peer in peers:
        pl.semaphore_signal(barrier, inc=1, device_id=peer, device_id_type=MESH)
    loads = [
        pltpu.make_async_copy(d_hbm, dv, in_s.at[0]),
        pltpu.make_async_copy(k_hbm, kv.at[0, c, x, pl.ds(0, T), pl.ds(0, W)], in_s.at[1]),
        pltpu.make_async_copy(v_hbm, kv.at[0, c, x, pl.ds(0, T), pl.ds(W, W)], in_s.at[2]),
        pltpu.make_async_copy(w_hbm, wz.at[z, c], in_s.at[3]),
        pltpu.make_async_copy(q_hbm, qv, in_s.at[4]),
    ]
    for load in loads:
        load.start()

    loads[1].wait()
    loads[2].wait()

    pl.semaphore_wait(barrier, len(peers))

    started = []

    def go(copy):
        copy.start()
        started.append((copy, None))

    def go_if(cond, copy):
        @pl.when(cond)
        def _():
            copy.start()
        started.append((copy, cond))

    def z_copy(p, half):
        rows = pl.ds(0, 96) if half == 0 else pl.ds(96, KVR - 96)
        return pltpu.make_async_remote_copy(
            src_ref=kv.at[p, c, x, rows], dst_ref=kv.at[p + 1, c, x, rows], send_sem=kvz_s.at[p, half],
            recv_sem=kvz_r.at[p, half], device_id=up, device_id_type=MESH)

    def x_start(p):
        blk = kv.at[p, c, x]
        go(rc(blk, kvx_s.at[p, 0], kvx_r.at[p, 0], right))
        go(rc(blk, kvx_s.at[p, 1], kvx_r.at[p, 1], left))
        go(rc(blk, kvd_s.at[p, 0], kvd_r.at[p, 0], sib))

    low, high = pl.ds(0, 96), pl.ds(96, KVR - 96)

    def x_relay(p):
        ref = kv.at[p, c, xl]
        rc(ref, kvx_s.at[p, 0], kvx_r.at[p, 0], right).wait_recv()
        go(rc(kv.at[p, c, xl, low], kvx_s.at[p, 2], kvx_r.at[p, 2], right))
        go(rc(ref, kvd_s.at[p, 1], kvd_r.at[p, 1], sib))
        ref = kv.at[p, c, xr]
        rc(ref, kvx_s.at[p, 1], kvx_r.at[p, 1], left).wait_recv()
        go(rc(kv.at[p, c, xr, high], kvx_s.at[p, 3], kvx_r.at[p, 3], left))
        go(rc(ref, kvd_s.at[p, 2], kvd_r.at[p, 2], sib))

    def x_end(p):
        rc(kv.at[p, c, xo, low], kvx_s.at[p, 2], kvx_r.at[p, 2], right).wait_recv()
        rc(kv.at[p, c, xo, high], kvx_s.at[p, 3], kvx_r.at[p, 3], left).wait_recv()
        go(rc(kv.at[p, c, xo], kvd_s.at[p, 3], kvd_r.at[p, 3], sib))

    def x_start_mixed(p, half):
        rows = (low, high)[half]
        for i, (to, dest) in enumerate(((right, xr), (left, xl), (across, xo))):
            go_if((x < dest) if p == 0 else (x > dest),
                  rc(kv.at[p, c, x, rows], kvm_s.at[p // 4, half, i], kvm_r.at[half, i], to))
        if half == 1:
            go_if(c == (0 if p == 0 else 1), rc(kv.at[p, c, x], kvd_s.at[p, 0], kvd_r.at[0, 0], sib))

    def plane_of(p, xx):
        return p if p > 0 else jnp.where(xx < x, 0, 4)

    def x_end_mixed():
        for i, xx in enumerate((xl, xr, xo)):
            ref = kv.at[plane_of(0, xx), c, xx]
            for half, rows in enumerate((low, high)):
                rc(ref.at[rows], kvm_s.at[0, half, i], kvm_r.at[half, i], right).wait_recv()
            go(rc(ref, kvd_s.at[0, i + 1], kvd_r.at[0, i + 1], sib))

    def sib_wait(p):
        own = p if p > 0 else jnp.where(c == 1, 0, 4)
        for i, (pp, xx) in enumerate(((own, x), (plane_of(p, xl), xl), (plane_of(p, xr), xr), (plane_of(p, xo), xo))):
            rc(kv.at[pp, oc, xx], kvd_s.at[p, i], kvd_r.at[p, i], sib).wait_recv()

    def z_step(p):
        for half in range(2):
            z_copy(p - 1, half).wait_recv()
            if p < DEPTH - 1:
                go(z_copy(p, half))
            else:
                x_start_mixed(p, half)
        if p < DEPTH - 1:
            x_start(p)

    def w_send(offset, i, dz):
        go(rc(wz.at[lax.rem(z + offset, NZ), c], wz_s.at[i], wz_r.at[i], dev(dz=dz)))

    def w_recv(i):
        ref = wz.at[lax.rem(z + i, NZ), c]
        rc(ref, wz_s.at[i], wz_r.at[i], up).wait_recv()
        go(rc(ref, wd_s.at[i], wd_r.at[i], sib))

    go(z_copy(0, 0))
    x_start_mixed(0, 0)

    loads[0].wait()
    docs = jnp.broadcast_to(dv[...], (W, T))
    number = lax.broadcasted_iota(jnp.int32, (W, T), 0)
    first = jnp.sum((docs < number).astype(F32), axis=1, keepdims=True)
    last = jnp.sum((docs <= number).astype(F32), axis=1, keepdims=True)
    first = jnp.transpose(jnp.broadcast_to(first, (W, W)))
    last = jnp.transpose(jnp.broadcast_to(last, (W, W)))
    stat = jnp.concatenate([first[0:8], last[0:8]], axis=0).astype(BF16)
    kv[0, c, x, T:KVR, 0:W] = stat
    kv[0, c, x, T:KVR, W:2 * W] = jnp.zeros((STAT, W), BF16)

    go(z_copy(0, 1))
    x_start_mixed(0, 1)
    loads[3].wait()
    w_send(0, 1, -1)
    w_send(0, 2, -2)
    go(rc(wz.at[z, c], wd_s.at[0], wd_r.at[0], sib))

    row = lax.broadcasted_iota(jnp.int32, (T, W), 0).astype(F32)

    def doc_rows(bounds):
        bounds = bounds.astype(F32)
        return jnp.where((row >= bounds[0:1]) & (row < bounds[8:9]), 1.0, 0.0)

    own_docs = doc_rows(stat)
    feature = jnp.where(own_docs > 0.5, 0.0, HIDE).astype(BF16)
    loads[4].wait()
    for u in range(2):
        for h in range(HEADS):
            rows = slice((u * HEADS + h) * HALF, (u * HEADS + h + 1) * HALF)
            qa[rows, 0:W] = qv[u * HALF:(u + 1) * HALF, h * W:(h + 1) * W]
            qa[rows, W:2 * W] = feature[u * HALF:(u + 1) * HALF]
    k_own = jnp.concatenate([kv[0, c, x, 0:T, 0:W], own_docs.astype(BF16)], axis=1)
    v_own = jnp.concatenate([kv[0, c, x, 0:T, W:2 * W], jnp.ones((T, W), BF16)], axis=1)
    wr[...] = jnp.zeros_like(wr)

    def diagonal(u):
        rows = slice(u * HEADS * HALF, (u + 1) * HEADS * HALF)
        at = lax.broadcasted_iota(jnp.int32, (HALF, T), 0) + u * HALF
        causal = at >= lax.broadcasted_iota(jnp.int32, (HALF, T), 1)
        scores = jnp.where(jnp.concatenate([causal] * HEADS, axis=0), dot_nt(qa[rows, :], k_own), -1e30)
        high = jnp.broadcast_to(jnp.max(scores, axis=1, keepdims=True) * SCALE, (HEADS * HALF, W))
        weights = jnp.exp2(scores * SCALE - high[:, 0:1]).astype(BF16)
        top[rows, :] = high
        acc[rows, :] = jnp.dot(weights, v_own, preferred_element_type=F32)

    def attend(blocks, valid, tile, after=None):
        count = len(blocks)
        for i, where in enumerate(blocks):
            docs_b = doc_rows(kv[where[0], where[1], where[2], T:KVR, 0:W])
            ff[i] = jnp.where(valid[i], docs_b, 1.0).astype(BF16)

        def score(u):
            keys = jnp.concatenate([kv[i[0], i[1], i[2], 0:T, 0:W] for i in blocks], axis=0)
            keys = jnp.concatenate([keys, ff[0:count].reshape(count * T, W)], axis=1)
            return dot_nt(qa[u * tile:(u + 1) * tile, :], keys)

        tiles = HEADS * T // tile
        ahead = score(0)
        for u in range(tiles):
            rows = slice(u * tile, (u + 1) * tile)
            scores = ahead
            if u + 1 < tiles:
                ahead = score(u + 1)
            old = top[rows, :]
            new = jnp.maximum(old, jnp.max(scores, axis=1, keepdims=True) * SCALE)
            weights = jnp.exp2(scores * SCALE - new[:, 0:1]).astype(BF16)
            vals = jnp.concatenate([kv[i[0], i[1], i[2], 0:T, W:2 * W] for i in blocks], axis=0)
            vals = jnp.concatenate([vals, jnp.ones((count * T, W), BF16)], axis=1)
            keep = jnp.exp2(old - new)
            acc[rows, :] = acc[rows, :] * jnp.concatenate([keep, keep], axis=1) + jnp.dot(
                weights, vals, preferred_element_type=F32)
            top[rows, :] = new
            if after is not None:
                after(u)

    def attend_plane(p):
        sib_wait(p)
        attend([(p, b // 4, b % 4) for b in range(8)], [z >= p] * 8, 320)

    def attend_mixed(core, after=None):
        early = [i * 2 + core < me for i in range(NX)]
        attend([(jnp.where(e, 0, 4), core, i) for i, e in enumerate(early)], [e | (z >= 4) for e in early], 480, after)

    def a_copy(u, i):
        return pltpu.make_async_remote_copy(
            src_ref=ag.at[0, pl.ds(u * HALF, HALF)], dst_ref=ag.at[1 + u, pl.ds(i * HALF, HALF)],
            send_sem=ax_s.at[u, i], recv_sem=ax_r.at[u, i], device_id=(right, left)[i], device_id_type=MESH)

    def a_send(u):
        mine = slice(u * HALF, (u + 1) * HALF)
        for h in range(HEADS):
            rows = slice((u * HEADS + h) * HALF, (u * HEADS + h + 1) * HALF)
            ag[0, mine, h * W:(h + 1) * W] = (acc[rows, 0:W] / acc[rows, W:2 * W]).astype(BF16)
        if u == 0:
            a_copy(0, 0).start()
            a_copy(0, 1).start()

    def a_far_copy(u, i):
        return pltpu.make_async_remote_copy(
            src_ref=ag.at[1 + u, pl.ds(i * (HALF + GROUP), GROUP)],
            dst_ref=ag.at[3, pl.ds(u * HALF + i * GROUP, GROUP)],
            send_sem=ax_s.at[u, 2 + i], recv_sem=ax_r.at[u, 2 + i],
            device_id=(right, left)[i], device_id_type=MESH)

    def a_near(u):
        for i in range(2):
            rc(ag.at[1 + u, pl.ds(i * HALF, HALF)], ax_s.at[u, i], ax_r.at[u, i], right).wait_recv()
            go(a_far_copy(u, i))

    def a_far():
        for u in range(2):
            for i in range(2):
                a_far_copy(u, i).wait_recv()

    def w_ready(i):
        plane = lax.rem(z + i, NZ)
        rc(wz.at[plane, oc], wd_s.at[i], wd_r.at[i], sib).wait_recv()
        for g in range(4):
            wr[plane, 32 * g:32 * g + 16, g * K:(g + 1) * K] = wz[plane, 0, 64:80, :]
            wr[plane, 32 * g + 16:32 * g + 32, g * K:(g + 1) * K] = wz[plane, 1, 64:80, :]

    z_step(1)
    diagonal(0)
    z_step(2)
    x_relay(1)
    z_step(3)
    w_send(0, 7, 1)
    w_send(0, 6, 2)
    diagonal(1)
    x_end(1)
    x_relay(2)
    w_recv(2)
    w_send(2, 3, -1)
    w_send(2, 4, -2)
    z_step(4)
    attend_plane(1)
    x_end(2)
    x_relay(3)
    attend_plane(2)
    x_end(3)
    w_recv(6)
    w_send(6, 5, 1)
    attend_plane(3)
    x_end_mixed()
    for i in (1, 7, 3, 4):
        w_recv(i)
    attend_mixed(c)
    w_recv(5)
    for i in (0, 1, 2, 3, 4, 6, 7):
        w_ready(i)
    sib_wait(0)
    attend_mixed(oc, a_send)
    w_ready(5)

    def partial(j, o):
        cols = jnp.concatenate([wz[o, 0, 0:64, :], wz[o, 1, 0:64, :]], axis=0)
        main = dot_nt(ag[j], cols)
        rows = jnp.concatenate([ag[j, g * GROUP:(g + 1) * GROUP, :] for g in range(4)], axis=1)
        rest = dot_nt(rows, wr[o])
        return jnp.concatenate([main[0:HALF], rest, main[HALF:T]], axis=0)

    y_up, y_down = dev(dy=1), dev(dy=-1)

    def hops(d, j):
        return 4 if (d + j) % 2 == 1 else 3

    def rs(d, r, j):
        return pltpu.make_async_remote_copy(
            src_ref=sbuf.at[d, r - 1, j], dst_ref=rbuf.at[d, r - 1, j],
            send_sem=rs_s.at[d, r - 1, j], recv_sem=rs_r.at[d, r - 1, j],
            device_id=dev(dy=1 if d == 0 else -1), device_id_type=MESH)

    def send_block(d, r, j, arrived):
        total = partial(j, lax.rem(t + r, NY) if d == 0 else lax.rem(t - r + NY, NY))
        for i in arrived:
            rs(d, i, j).wait_recv()
            total = total + rbuf[d, i - 1, j].astype(F32)
        sbuf[d, r - 1, j] = total.astype(BF16)
        go(rs(d, r, j))

    def send_step(n, j):
        for d in range(2):
            r = hops(d, j) - n
            arrived = () if n == 0 else (r + 1,)
            if r > 0:
                send_block(d, r, j, arrived)

    def fx(j, i):
        to, slot, half = ((), ((left, 1, 0), (right, 3, 0)), ((left, 1, 1), (right, 3, 1)), ((across, 2, 0), (across, 2, 1)))[j][i]
        return pltpu.make_async_remote_copy(
            src_ref=fsend.at[j - 1, pl.ds(i * HALF, HALF + GROUP)], dst_ref=fin.at[slot, half],
            send_sem=fx_s.at[2 * slot + half - 2], recv_sem=fx_r.at[2 * slot + half - 2],
            device_id=to, device_id_type=MESH)

    def finish(j):
        total = partial(j, t)
        for d in range(2):
            rs(d, 1, j).wait_recv()
            total = total + rbuf[d, 0, j].astype(F32)
        total = total.astype(BF16)
        if j == 0:
            fin[0, 0] = total[0:HALF + GROUP]
            fin[0, 1] = total[HALF:PACK]
        else:
            fsend[j - 1] = total
            go(fx(j, 0))
            go(fx(j, 1))

    def second(slot, half):
        return slot == 3 or (slot != 1 and half == 1)

    send_step(0, 0)
    for i in range(2):
        a_copy(0, i).wait_send()
        go(a_copy(1, i))
    a_near(0)
    send_step(0, 1)

    lane = lax.broadcasted_iota(jnp.int32, (W, K), 0)
    spot = lax.rem(lane, 32)
    main_at = lane + jnp.where(lane < 64, 0, 16)
    rest_at = spot + jnp.where(spot < 16, 64, 128)
    for i in range(NX):
        col = lax.broadcasted_iota(jnp.int32, (W, K), 1) - lax.rem(x + i, NX) * 160
        rows = slice(i * W, (i + 1) * W)
        selm[rows, :] = jnp.where(col == main_at, 1.0, 0.0).astype(BF16)
        for u in range(2):
            for g in range(2):
                here = lane // 32 == g + (2 if second(i, u) else 0)
                selr[2 * u + g, rows, :] = jnp.where((col == rest_at) & here, 1.0, 0.0).astype(BF16)

    send_step(1, 0)
    a_near(1)
    send_step(0, 2)
    send_step(1, 1)
    send_step(2, 0)
    a_far()
    send_step(0, 3)
    send_step(1, 2)
    send_step(2, 1)
    send_step(1, 3)
    send_step(2, 2)
    send_step(3, 1)
    send_step(2, 3)
    send_step(3, 2)
    send_step(3, 3)
    send_step(3, 0)
    finish(1)
    finish(3)
    finish(2)
    finish(0)

    def main_of(i, u):
        return fin[i, u, GROUP:GROUP + HALF, :] if second(i, u) else fin[i, u, 0:HALF, :]

    def rest_of(i, u):
        return fin[i, u, 0:GROUP, :] if second(i, u) else fin[i, u, HALF:HALF + GROUP, :]

    def place(slots):
        lanes = slice(slots[0] * W, (slots[-1] + 1) * W)
        halves = []
        for u in range(2):
            main = jnp.dot(jnp.concatenate([main_of(i, u) for i in slots], axis=1), selm[lanes, :], preferred_element_type=F32)
            rest = jnp.concatenate([rest_of(i, u) for i in slots], axis=1)
            add = [jnp.dot(rest, selr[2 * u + g, lanes, :], preferred_element_type=F32) for g in range(2)]
            halves.append(main + jnp.concatenate(add, axis=0))
        return jnp.concatenate(halves, axis=0)

    for i in range(2):
        fx(3, i).wait_recv()
    out[...] = place((2,))
    fx(1, 0).wait_recv()
    fx(2, 0).wait_recv()
    out[...] += place((0, 1))
    fx(1, 1).wait_recv()
    fx(2, 1).wait_recv()
    o_ref[...] = (out[...] + place((3,))).astype(BF16)

    for copy, cond in started:
        if cond is None:
            copy.wait_send()
        else:
            pl.when(cond)(copy.wait_send)


def local(queries, keys, values, doc_ids, w_out):
    sem = pltpu.SemaphoreType.DMA
    vmem = pl.BlockSpec(memory_space=pltpu.VMEM)
    return pl.pallas_call(
        kernel,
        out_shape=pltpu.VMEM((T, K), BF16),
        in_specs=[pl.BlockSpec(memory_space=pl.ANY)] * 5,
        out_specs=vmem,
        scratch_shapes=[
            pltpu.VMEM((DEPTH, 2, NX, KVR, 2 * W), BF16),
            pltpu.VMEM((8, T, W), BF16),
            pltpu.VMEM((T, K), BF16),
            pltpu.VMEM((1, T), jnp.int32),
            pltpu.VMEM((HEADS * T, 2 * W), BF16),
            pltpu.VMEM((HEADS * T, 2 * W), F32),
            pltpu.VMEM((HEADS * T, W), F32),
            pltpu.VMEM((NZ, 2, COLS, K), BF16),
            pltpu.VMEM((NY, W, 4 * K), BF16),
            pltpu.VMEM((NX, T, K), BF16),
            pltpu.VMEM((2, 4, NX, PACK, W), BF16),
            pltpu.VMEM((2, 4, NX, PACK, W), BF16),
            pltpu.VMEM((3, PACK, W), BF16),
            pltpu.VMEM((NX, 2, HALF + GROUP, W), BF16),
            pltpu.VMEM((NX * W, K), BF16),
            pltpu.VMEM((4, NX * W, K), BF16),
            pltpu.VMEM((T, K), F32),
            sem((5,)), sem((4, 2)), sem((4, 2)), sem((4, 4)), sem((4, 4)), sem((2, 2, 3)), sem((2, 3)), sem((5, 4)), sem((5, 4)),
            sem((8,)), sem((8,)), sem((8,)), sem((8,)),
            sem((2, 4)), sem((2, 4)), sem((2, 4, NX)), sem((2, 4, NX)), sem((6,)), sem((6,)),
        ],
        compiler_params=pltpu.CompilerParams(
            collective_id=0, has_side_effects=True, vmem_limit_bytes=56 * 2**20),
        name="attend_project",
    )(queries, keys, values, doc_ids.reshape(1, T), w_out.T)


def solution(mesh):
    placed = (P("seq", "tp"), P("seq", "tp"), P("seq", "tp"), P("seq"), P("tp", "seq"))
    return jax.shard_map(
        local, mesh=mesh, in_specs=placed, out_specs=P("seq", "tp"), check_vma=False
    )
```
